256 devices in a mesh: tm: 32 (over y, z), space: 8 (over x, core).
Axes of the slice: x: 4, y: 4, z: 8, core: 2. Of those that a mesh axis runs over, the one named last changes fastest.
Arguments:
- source: float32 [256, 320, 64], P('tm', None, 'space'), may hold values from -21 to 21
- decay_rate: float32 [256, 320, 64], P('tm', None, 'space'), may hold values from 0.4 to 1
- blocks: bfloat16 [64, 7, 102400], P('space'), may hold values from -0.0048828125 to 0.0048828125
- neighbours: int32 [6, 64], P(None, 'space'), may hold values from 0 to 7
- interface_jacobian_blocks: bfloat16 [2, 16, 102400], P(None, 'space'), may hold values from -0.0048828125 to 0.0048828125
- face_element_owner: int32 [2, 16], P(None, 'space'), may hold values from 0 to 7
- pairing: int32 [8, 2], P('space'), may hold values from 0 to 1, each once within a row
Outputs:
- adjoint: float32 [256, 320, 64], P('tm', None, 'space')
- residual: float32 [256, 320, 64], P('tm', None, 'space')
The draws below stay inside these ranges and needn't reach their ends.
Inputs may be any that keep to these rules, and one draw needn't show every extreme that they name: `neighbours`: element indices local to the element's own partition. `face_element_owner`: element indices local to the slot's own partition. `pairing`: each row is a permutation of 0 to 1.
All inputs are finite; a program needn't handle non-finite values.
Results may differ from the reference program's by a relative error of at most 0.0003.
Values sent between devices are 32-bit elements; how exact they have to be, the bound alone decides.
No kernel may reach another device: no remote copies, remote signals or barrier semaphores. Data moves between devices by JAX's collectives and lax.ppermute only.
A program may use at most 128 MiB of HBM per device.

```python
import jax
import jax.numpy as jnp
from jax import lax

BLOCK_UNKNOWNS = 320
NF = 6
PART_ELEMENTS = 8
NI = 2
TIME_SLABS = 256
NEL = 64
NPART = 8
INTERFACE_SLOTS = 16


def draw_source(key, part):
    key = jax.random.fold_in(key, 11)
    random_child_keys = jax.random.split(key, 2)
    full_shape = (TIME_SLABS, BLOCK_UNKNOWNS, NEL)
    slab_pos = jnp.arange(TIME_SLABS, dtype=jnp.float32)[:, None, None] / TIME_SLABS
    elem_pos = (jnp.arange(NEL) // PART_ELEMENTS).astype(jnp.float32)[None, None, :] / NPART
    rising = (0.7 + 0.6 * slab_pos) * (0.7 + 0.6 * elem_pos)
    spread = jnp.exp(jax.random.uniform(random_child_keys[1], (1, BLOCK_UNKNOWNS, NEL), minval=jnp.log(0.3), maxval=jnp.log(3.0)))
    values = jnp.clip(jax.random.normal(random_child_keys[0], full_shape), -4.0, 4.0)
    return (values * spread * rising).astype(jnp.float32)


def draw_decay_rate(key, part):
    key = jax.random.fold_in(key, 23)
    random_child_keys = jax.random.split(key, 5)
    full_shape = (TIME_SLABS, BLOCK_UNKNOWNS, NEL)
    slow_count = 5
    gradual_slab_mask = jax.random.randint(random_child_keys[0], (1, BLOCK_UNKNOWNS, NEL), 0, 10) < slow_count
    lasting = jax.random.uniform(random_child_keys[1], (1, BLOCK_UNKNOWNS, NEL), minval=0.7, maxval=1.6)
    jitter = jax.random.uniform(random_child_keys[2], full_shape, minval=0.0, maxval=0.3)
    gradual_decay_rate = jnp.exp(-(lasting + jitter) / TIME_SLABS)
    quick_decay_rate = jax.random.uniform(random_child_keys[3], full_shape, minval=0.4, maxval=0.8)
    rapid_slab_count = jax.random.randint(random_child_keys[4], (2,), 0, TIME_SLABS)
    time_slab_index = jnp.arange(TIME_SLABS)[:, None, None]
    rapid_decay = jnp.where((time_slab_index == rapid_slab_count[0]) | (time_slab_index == rapid_slab_count[1]), 0.75, 1.0)
    return jnp.where(gradual_slab_mask, gradual_decay_rate * rapid_decay, quick_decay_rate).astype(jnp.float32)


def plant(array, key, smallest, top_value):
    index_at = [jax.random.randint(jax.random.fold_in(key, axis), (), 0, length) for axis, length in enumerate(array.shape)]
    longest = array.shape.index(max(array.shape))
    beside = index_at[:longest] + [(index_at[longest] + 1) % array.shape[longest]] + index_at[longest + 1:]
    return array.at[tuple(index_at)].set(smallest).at[tuple(beside)].set(top_value)


def level_of(stream_key, extent, shards, least, largest):
    level = 1.0
    for dim, parts in shards:
        draws = jax.random.uniform(jax.random.fold_in(jax.random.fold_in(stream_key, 6), dim), (parts,), jnp.float32, least / len(shards), largest / len(shards))
        level = level * jnp.repeat(jnp.exp(draws), extent[dim] // parts).reshape((-1,) + (1,) * (len(extent) - 1 - dim))
    return level


def bell_draw(own_key, extent, scale, bound, cuts=(), kind=jnp.bfloat16):
    drawn = scale * jax.random.normal(own_key, extent, jnp.float32)
    if cuts:
        drawn = drawn * level_of(own_key, extent, cuts, -0.22, 0.18)
    return jnp.clip(drawn, -bound, bound).astype(kind)


def setup_inputs(seed: int = 0) -> dict:
    arg_keys = jax.random.split(jax.random.key(seed), 8)
    source = draw_source(jax.random.fold_in(arg_keys[7], 71), 0)
    decay_rate = draw_decay_rate(jax.random.fold_in(arg_keys[7], 71), 0)
    blocks = bell_draw(arg_keys[2], (NEL, NF + 1, BLOCK_UNKNOWNS * BLOCK_UNKNOWNS), (BLOCK_UNKNOWNS * 16 * TIME_SLABS) ** -0.5, 0.0048828125, ((0, 8),))
    neighbours = plant(jax.random.randint(arg_keys[3], (NF, NEL), 0, PART_ELEMENTS), jax.random.fold_in(arg_keys[3], 1), 0, PART_ELEMENTS - 1).astype(jnp.int32)
    interface_jacobian_blocks = bell_draw(arg_keys[4], (2, INTERFACE_SLOTS, BLOCK_UNKNOWNS * BLOCK_UNKNOWNS), (BLOCK_UNKNOWNS * 16 * TIME_SLABS) ** -0.5, 0.0048828125, ((1, 8),))
    face_element_owner = plant(jax.random.randint(arg_keys[5], (2, INTERFACE_SLOTS), 0, PART_ELEMENTS), jax.random.fold_in(arg_keys[5], 1), 0, PART_ELEMENTS - 1).astype(jnp.int32)
    pairing = jax.vmap(lambda own: jax.random.permutation(own, NI))(jax.random.split(arg_keys[6], NPART)).reshape((NPART, NI)).astype(jnp.int32)
    return {"source": source, "decay_rate": decay_rate, "blocks": blocks, "neighbours": neighbours, "interface_jacobian_blocks": interface_jacobian_blocks, "face_element_owner": face_element_owner, "pairing": pairing}


epsilon = 1e-06

def periodic_chain(field, decay_rate):

    def compose_step(carry, inputs):
        product, offset = carry
        slab_rate, slab_value = inputs
        return ((product * slab_rate, slab_value + slab_rate * offset), None)
    initial = (jnp.ones(field.shape[1:], jnp.float32), jnp.zeros(field.shape[1:], jnp.float32))
    (product, offset), unused = lax.scan(compose_step, initial, (decay_rate, field), reverse=True)
    closing = offset / (1.0 - product)

    def sweep_step(carried, inputs):
        slab_rate, slab_value = inputs
        carried = slab_value + slab_rate * carried
        return (carried, carried)
    unused_last, solved = lax.scan(sweep_step, closing, (decay_rate, field), reverse=True)
    return solved

def spatial(slab_field, block_lead, neighbour_ids, coupling_leading, upper_ids, lower_ids, pairing, down_dest):
    contribs = jnp.einsum('efnm,ne->fme', block_lead, slab_field, precision=lax.Precision.HIGHEST)
    result = contribs[0]
    for face in range(neighbour_ids.shape[0]):
        result = result.at[:, neighbour_ids[face]].add(contribs[face + 1])
    upward = jnp.einsum('inm,ni->mi', coupling_leading[0], slab_field[:, upper_ids.reshape(-1)], precision=lax.Precision.HIGHEST)
    downward = jnp.einsum('inm,ni->mi', coupling_leading[1], slab_field[:, lower_ids.reshape(-1)], precision=lax.Precision.HIGHEST)
    shifted = jnp.roll(upward.reshape(BLOCK_UNKNOWNS, NPART, NI), 1, axis=1)
    received = jnp.take_along_axis(shifted, pairing[None, :, :], axis=2)
    result = result.at[:, lower_ids.reshape(-1)].add(received.reshape(BLOCK_UNKNOWNS, NPART * NI))
    return result.at[:, down_dest.reshape(-1)].add(downward)

def reference(source, decay_rate, blocks, neighbours, interface_jacobian_blocks, face_element_owner, pairing):
    block_lead = blocks.astype(jnp.float32).reshape(NEL, NF + 1, BLOCK_UNKNOWNS, BLOCK_UNKNOWNS)
    coupling_leading = interface_jacobian_blocks.astype(jnp.float32).reshape(2, INTERFACE_SLOTS, BLOCK_UNKNOWNS, BLOCK_UNKNOWNS)
    owner_base = jnp.arange(NEL, dtype=jnp.int32) // PART_ELEMENTS * PART_ELEMENTS
    neighbour_ids = neighbours + owner_base[None, :]
    part_base = (jnp.arange(NPART, dtype=jnp.int32) * PART_ELEMENTS)[:, None]
    upper_ids = face_element_owner[0].reshape(NPART, NI) + part_base
    lower_ids = face_element_owner[1].reshape(NPART, NI) + part_base
    down_dest = jnp.take_along_axis(jnp.roll(upper_ids, 1, axis=0), pairing, axis=1)

    def operate(current):
        chained = periodic_chain(current, decay_rate)
        coupled = lax.map(lambda slab_field: spatial(slab_field, block_lead, neighbour_ids, coupling_leading, upper_ids, lower_ids, pairing, down_dest), chained)
        return (chained, current + coupled)
    norm_source = jnp.sqrt(jnp.sum(source * source) + epsilon)
    first_vec = source / norm_source
    first_sol, first_out = operate(first_vec)
    along_first = jnp.sum(first_vec * first_out)
    first_rest = first_out - along_first * first_vec
    height_one = jnp.sqrt(jnp.sum(first_rest * first_rest) + epsilon)
    second_vec = first_rest / height_one
    second_sol, second_out = operate(second_vec)
    cross_first = jnp.sum(first_vec * second_out)
    along_second = jnp.sum(second_vec * second_out)
    second_rest = second_out - cross_first * first_vec - along_second * second_vec
    height_two = jnp.sqrt(jnp.sum(second_rest * second_rest) + epsilon)
    radius_one = jnp.sqrt(along_first * along_first + height_one * height_one)
    cosine_one = along_first / radius_one
    sine_one = height_one / radius_one
    upper_right = cosine_one * cross_first + sine_one * along_second
    pivot_two = cosine_one * along_second - sine_one * cross_first
    radius_two = jnp.sqrt(pivot_two * pivot_two + height_two * height_two)
    weight_two = -(norm_source * sine_one) * (pivot_two / radius_two) / radius_two
    weight_one = (norm_source * cosine_one - upper_right * weight_two) / radius_one
    adjoint = weight_one * first_sol + weight_two * second_sol
    residual = source - weight_one * first_out - weight_two * second_out
    return (adjoint, residual)
```

```python
import jax
import jax.numpy as jnp
from jax import lax
from jax.experimental import pallas as pl
from jax.experimental.pallas import tpu as pltpu
from jax.sharding import PartitionSpec as P

EPSILON = 1e-06
F32 = jnp.float32
BF16 = jnp.bfloat16
SLABS = 8
ELEMENTS = 8
WIDTH = 320
FACES = 7
ROWS = SLABS * ELEMENTS
PAIRS = WIDTH // 2
DEPTH = PAIRS * ELEMENTS
LANES = 2 * WIDTH
GROUPS = 32
DEVICES = 256
TINY = 1e-30

VMEM = pl.BlockSpec(memory_space=pltpu.VMEM)
SMEM = pl.BlockSpec(memory_space=pltpu.SMEM)
ANY = pl.BlockSpec(memory_space=pl.ANY)


def iota(shape, dim):
    return lax.broadcasted_iota(jnp.int32, shape, dim)


def struct(*shape):
    return jax.ShapeDtypeStruct(shape, F32)


def params(mib):
    return pltpu.CompilerParams(vmem_limit_bytes=mib * 1024 * 1024)


def maps_kernel(source_ref, decay_ref, out_ref):
    product = jnp.ones((ELEMENTS, WIDTH), F32)
    offset = jnp.zeros((ELEMENTS, WIDTH), F32)
    for t in reversed(range(SLABS)):
        offset = source_ref[t] + decay_ref[t] * offset
        product = product * decay_ref[t]
    for j in range(GROUPS):
        out_ref[j, 0:ELEMENTS] = product
        out_ref[j, ELEMENTS:] = offset


def entering_value(mine, product_of, offset_of):
    product = jnp.ones((ELEMENTS, WIDTH), F32)
    offset = jnp.zeros((ELEMENTS, WIDTH), F32)
    for j in reversed(range(GROUPS)):
        offset = offset_of(j) + product_of(j) * offset
        product = product * product_of(j)
    value = offset / (1.0 - product)
    for j in reversed(range(1, GROUPS)):
        value = jnp.where(j > mine, offset_of(j) + product_of(j) * value, value)
    return value


def operate_kernel(first, *refs):
    if first:
        mine, neighbours, owner, pairing, field, decay, maps, blocks, couple = refs[:9]
        refs = refs[9:]
        offset_of = lambda j: maps[j, ELEMENTS:]
    else:
        mine, neighbours, owner, pairing, field, decay, maps, offsets, blocks, couple = refs[:10]
        refs = refs[10:]
        offset_of = lambda j: offsets[j]
    chained, local, up, down, raw, weights, spread, total, sems = refs
    copies = [
        pltpu.make_async_copy(blocks.at[f], raw.at[f], sems.at[f]) for f in range(FACES)
    ]
    for copy in copies:
        copy.start()

    value = entering_value(mine[0], lambda j: maps[j, 0:ELEMENTS], offset_of)
    for t in reversed(range(SLABS)):
        value = field[t] + decay[t] * value
        chained[t] = value
    z = chained[...].reshape(ROWS, WIDTH)
    high = z.astype(BF16)
    low = (z - high.astype(F32)).astype(BF16)
    parts = jnp.concatenate([high, low], axis=0)

    row = iota((4 * 2 * SLABS, 2 * ROWS), 0)
    col = iota((4 * 2 * SLABS, 2 * ROWS), 1)
    slot = row // (2 * SLABS)
    at = jnp.where(
        slot < 2,
        jnp.where(slot == 0, owner[0, 0], owner[0, 1]),
        jnp.where(slot == 2, owner[1, 0], owner[1, 1]),
    )
    pick = (row % (2 * SLABS)) * ELEMENTS + at == col
    pick = jnp.where(pick, 1.0, 0.0).astype(BF16)
    picked = jnp.dot(pick, parts, preferred_element_type=F32).astype(BF16)
    for side in range(2):
        for i in range(2):
            k = (2 * side + i) * 2 * SLABS
            both = jnp.dot(
                picked[k : k + 2 * SLABS], couple[side, i], preferred_element_type=F32
            )
            both = both[:SLABS] + both[SLABS:]
            if side == 0:
                up[i] = both
            else:
                down[pairing[0, i]] = both

    span = 1024
    n = iota((256, span), 0)
    lane = iota((256, span), 1)
    same = jnp.where(iota((128, 128), 0) // 8 == iota((128, 128), 1) // 8, 1.0, 0.0).astype(BF16)
    own = iota((2 * ROWS, DEPTH), 0) % ELEMENTS == iota((2 * ROWS, DEPTH), 1) % ELEMENTS
    for b in range(2):
        expand = jnp.where(n == 2 * (lane // ELEMENTS) + b, 1.0, 0.0).astype(BF16)
        wide = jnp.concatenate(
            [
                jnp.dot(parts[:, :256], expand, preferred_element_type=F32),
                jnp.dot(parts[:, 256:], expand[:64, :256], preferred_element_type=F32),
            ],
            axis=1,
        )
        wide = jnp.where(own, wide, 0.0).astype(BF16)
        spread[b * 2 * ROWS : (b + 1) * 2 * ROWS] = jnp.dot(
            same, wide, preferred_element_type=F32
        ).astype(BF16)

    total[...] = jnp.zeros_like(total)
    e = iota((2 * ELEMENTS, 128), 1) % ELEMENTS
    d = iota((2 * ELEMENTS, 128), 0) % ELEMENTS

    def face(f, carry):
        pltpu.make_async_copy(blocks.at[f], raw.at[f], sems.at[f]).wait()
        to = e
        for k in range(ELEMENTS):
            to = jnp.where((e == k) & (f > 0), neighbours[jnp.maximum(f - 1, 0), k], to)
        mask = jnp.where(to == d, 1.0, 0.0).astype(BF16)
        mask = jnp.concatenate([mask] * (DEPTH // 128), axis=1)
        mask = jnp.concatenate([mask] * (4 * ROWS // 16), axis=0)
        for k in range(PAIRS // 2):
            two = [
                raw[f, :, (2 * k + i) * LANES : (2 * k + i + 1) * LANES].astype(F32)
                for i in range(2)
            ]
            weights[k * 16 : (k + 1) * 16] = jnp.concatenate(two, axis=0).astype(BF16)
        total[...] += jnp.dot(spread[...] * mask, weights[...], preferred_element_type=F32)
        return carry

    lax.fori_loop(0, FACES, face, 0)
    result = (
        total[0:ROWS, :WIDTH]
        + total[ROWS : 2 * ROWS, :WIDTH]
        + (total[2 * ROWS : 3 * ROWS, :] + total[3 * ROWS :, :])[:, WIDTH:]
    )
    local[...] = result.reshape(SLABS, ELEMENTS, WIDTH)


def operate(first, scalars, field, decay, gathered, blocks, couple):
    def kernel(*refs):
        operate_kernel(first, *refs)

    return pl.pallas_call(
        kernel,
        out_shape=(
            struct(SLABS, ELEMENTS, WIDTH),
            struct(SLABS, ELEMENTS, WIDTH),
            struct(2, SLABS, WIDTH),
            struct(2, SLABS, WIDTH),
        ),
        in_specs=[SMEM] * 4 + [VMEM] * (2 + len(gathered)) + [ANY, VMEM],
        out_specs=(VMEM,) * 4,
        scratch_shapes=[
            pltpu.VMEM((FACES, ELEMENTS, WIDTH * WIDTH), BF16),
            pltpu.VMEM((DEPTH, LANES), BF16),
            pltpu.VMEM((4 * ROWS, DEPTH), BF16),
            pltpu.VMEM((4 * ROWS, LANES), F32),
            pltpu.SemaphoreType.DMA((FACES,)),
        ],
        compiler_params=params(48),
    )(*scalars, field, decay, *gathered, blocks, couple)


def add_halo(owner, pairing, local, below, above, out):
    at = iota((ELEMENTS, WIDTH), 0)
    for t in range(SLABS):
        value = local[t]
        for k in range(2):
            value = value + jnp.where(
                at == owner[1, k], below[pairing[0, k], pl.ds(t, 1)], 0.0
            )
            value = value + jnp.where(at == owner[0, k], above[k, pl.ds(t, 1)], 0.0)
        out[t] = value


def middle_kernel(owner, pairing, local, below, above, decay, image, out):
    add_halo(owner, pairing, local, below, above, image)
    offset = jnp.zeros((ELEMENTS, WIDTH), F32)
    for t in reversed(range(SLABS)):
        offset = image[t] + decay[t] * offset
    for j in range(GROUPS):
        out[j] = offset


def total_of(x):
    return jnp.sum(jnp.sum(x, axis=0), keepdims=True)


def gram_kernel(owner, pairing, local, below, above, source, image0, image1, out):
    add_halo(owner, pairing, local, below, above, image1)
    s = source[...]
    largest = [
        jnp.maximum(jnp.max(jnp.max(jnp.abs(image[...]), axis=0), keepdims=True), TINY)
        for image in (image0, image1)
    ]
    one = jnp.ones((1, 1), F32)
    g0 = image0[...] * (1.0 / largest[0])
    g1 = image1[...] * (1.0 / largest[1])
    entries = [
        (total_of(s * s), one, one),
        (total_of(s * g0), largest[0], one),
        (total_of(g0 * g0), largest[0], largest[0]),
        (total_of(s * g1), largest[1], one),
        (total_of(g0 * g1), largest[0], largest[1]),
        (total_of(g1 * g1), largest[1], largest[1]),
    ]
    lane = iota((8, 128), 1)
    row = jnp.ones((8, 128), F32)
    for k, entry in enumerate(entries):
        for i, value in enumerate(entry):
            row = jnp.where(lane == k + 16 * i, value, row)
    for j in range(DEVICES // 8):
        out[j * 8 : (j + 1) * 8] = row


def last_kernel(gram, source, first_chain, second_chain, image0, image1, adjoint, residual):
    every = gram[...]
    scale_a = pltpu.roll(every, 128 - 16, 1)
    scale_b = pltpu.roll(every, 128 - 32, 1)
    top_a = jnp.max(scale_a, axis=0, keepdims=True)
    top_b = jnp.max(scale_b, axis=0, keepdims=True)
    sums = jnp.sum(every * (scale_a / top_a) * (scale_b / top_b), axis=0, keepdims=True)
    lane = iota((1, 128), 1)

    def entry(row, k):
        return jnp.sum(jnp.where(lane == k, row, 0.0), axis=1, keepdims=True)

    ss, s0, g00, s1, g01, g11 = (entry(sums, k) for k in range(6))
    a0 = entry(top_a, 1)
    a1 = entry(top_a, 3)
    square = ss + EPSILON
    norm = jnp.sqrt(square)
    r0 = a0 / norm
    kappa = EPSILON / square - r0 * (s0 / norm)
    rest = r0 * r0 * g00 + 2.0 * kappa * r0 * (s0 / norm) + kappa * kappa * (ss / square)
    h10 = jnp.sqrt(jnp.maximum(rest, 0.0) + EPSILON)
    beta = 1.0 / (norm * h10)
    b0 = r0 / h10
    b1 = (a1 / norm) / h10
    cross = b0 * b1 * g01 + kappa * beta * b1 * s1
    delta = cross + kappa * (b0 * b0 * g00 + kappa * beta * b0 * s0)
    lost = EPSILON / (h10 * h10)
    h00 = 1.0 - kappa
    h11 = (1.0 - lost) + delta
    near = EPSILON * (1.0 - kappa) * beta
    h01 = (b1 * s1 + kappa * b0 * s0 + near) / norm
    c1 = kappa + lost - delta
    mu = (b1 * s1 + beta * EPSILON) / square
    rest = (
        b1 * b1 * g11
        + c1 * c1 * (1.0 - lost)
        + mu * mu * ss
        + 2.0 * c1 * cross
        - 2.0 * mu * b1 * s1
        - 2.0 * c1 * mu * near
    )
    h21 = jnp.sqrt(jnp.maximum(rest, 0.0) + EPSILON)
    radius_one = jnp.sqrt(h00 * h00 + h10 * h10)
    cosine = h00 / radius_one
    sine = h10 / radius_one
    upper = cosine * h01 + sine * h11
    pivot = cosine * h11 - sine * h01
    radius_two = jnp.sqrt(pivot * pivot + h21 * h21)
    y1 = -(norm * sine) * (pivot / radius_two) / radius_two
    y0 = (norm * cosine - upper * y1) / radius_one
    p0 = y0 / norm
    p1 = y1 * beta
    p2 = p1 * kappa
    for t in range(SLABS):
        adjoint[t] = (p0 + p2) * first_chain[t] + p1 * second_chain[t]
        residual[t] = (
            (1.0 - p0 - p2) * source[t] - (p0 + p1 + p2) * image0[t] - p1 * image1[t]
        )


def shards(
    source, decay_rate, blocks, neighbours, interface_jacobian_blocks, face_element_owner, pairing
):
    source = jnp.transpose(source, (0, 2, 1))
    decay = jnp.transpose(decay_rate, (0, 2, 1))
    blocks = jnp.transpose(blocks, (1, 0, 2))
    couple = interface_jacobian_blocks.reshape(2, 2, WIDTH, WIDTH)
    mine = lax.axis_index("tm").astype(jnp.int32).reshape(1)
    scalars = (mine, neighbours, face_element_owner, pairing)
    owner_pairing = (face_element_owner, pairing)
    field_shape = struct(SLABS, ELEMENTS, WIDTH)
    upward = [(i, (i + 1) % 8) for i in range(8)]
    downward = [((i + 1) % 8, i) for i in range(8)]

    maps = pl.pallas_call(
        maps_kernel,
        out_shape=struct(GROUPS, 2 * ELEMENTS, WIDTH),
        in_specs=[VMEM] * 2,
        out_specs=VMEM,
    )(source, decay)
    maps = lax.all_to_all(maps, "tm", 0, 0, tiled=True)
    chain0, local, up, down = operate(True, scalars, source, decay, (maps,), blocks, couple)
    below = lax.ppermute(up, "space", upward)
    above = lax.ppermute(down, "space", downward)
    image0, offsets = pl.pallas_call(
        middle_kernel,
        out_shape=(field_shape, struct(GROUPS, ELEMENTS, WIDTH)),
        in_specs=[SMEM] * 2 + [VMEM] * 4,
        out_specs=(VMEM,) * 2,
    )(*owner_pairing, local, below, above, decay)
    offsets = lax.all_to_all(offsets, "tm", 0, 0, tiled=True)
    chain1, local, up, down = operate(
        False, scalars, image0, decay, (maps, offsets), blocks, couple
    )
    below = lax.ppermute(up, "space", upward)
    above = lax.ppermute(down, "space", downward)
    image1, gram = pl.pallas_call(
        gram_kernel,
        out_shape=(field_shape, struct(DEVICES, 128)),
        in_specs=[SMEM] * 2 + [VMEM] * 5,
        out_specs=(VMEM,) * 2,
    )(*owner_pairing, local, below, above, source, image0)
    gram = lax.all_to_all(gram, ("tm", "space"), 0, 0, tiled=True)
    adjoint, residual = pl.pallas_call(
        last_kernel,
        out_shape=(field_shape, field_shape),
        in_specs=[VMEM] * 6,
        out_specs=(VMEM,) * 2,
    )(gram, source, chain0, chain1, image0, image1)
    return (jnp.transpose(adjoint, (0, 2, 1)), jnp.transpose(residual, (0, 2, 1)))


def solution(mesh):
    in_specs = (
        P("tm", None, "space"),
        P("tm", None, "space"),
        P("space", None, None),
        P(None, "space"),
        P(None, "space", None),
        P(None, "space"),
        P("space", None),
    )
    out_specs = (P("tm", None, "space"), P("tm", None, "space"))
    return jax.shard_map(shards, mesh=mesh, in_specs=in_specs, out_specs=out_specs, check_vma=False)
```

```python
import jax
import jax.numpy as jnp
from jax import lax
from jax.experimental import pallas as pl
from jax.experimental.pallas import tpu as pltpu
from jax.sharding import PartitionSpec as P

EPSILON = 1e-06
F32 = jnp.float32
BF16 = jnp.bfloat16
SLABS = 8
ELEMENTS = 8
WIDTH = 320
FACES = 7
ROWS = SLABS * ELEMENTS
PAIRS = WIDTH // 2
DEPTH = PAIRS * ELEMENTS
LANES = 2 * WIDTH
RING = 8
LINES = 4
DEVICES = 256
TINY = 1e-30
SPAN = 1024
SMALL_MIB = 4
OPERATE_MIB = 8
WIDE_MIB = 46
RESIDENT = (True, True)
WHOLE_MIB = 54

VMEM = pl.BlockSpec(memory_space=pltpu.VMEM)
SMEM = pl.BlockSpec(memory_space=pltpu.SMEM)
HBM = pl.BlockSpec(memory_space=pltpu.HBM)


def iota(shape, dim):
    return lax.broadcasted_iota(jnp.int32, shape, dim)


def struct(*shape):
    return jax.ShapeDtypeStruct(shape, F32)


def params(mib):
    return pltpu.CompilerParams(vmem_limit_bytes=mib * 1024 * 1024)


def maps_kernel(source_ref, decay_ref, out_ref, source, decay, sems):
    copies = [
        pltpu.make_async_copy(source_ref, source, sems.at[0]),
        pltpu.make_async_copy(decay_ref, decay, sems.at[1]),
    ]
    for copy in copies:
        copy.start()
    for copy in copies:
        copy.wait()
    product = jnp.ones((ELEMENTS, WIDTH), F32)
    offset = jnp.zeros((ELEMENTS, WIDTH), F32)
    for t in reversed(range(SLABS)):
        offset = source[t] + decay[t] * offset
        product = product * decay[t]
    for j in range(RING):
        out_ref[j, 0:ELEMENTS] = product
        out_ref[j, ELEMENTS:] = offset


def prepare_kernel(
    mine,
    neighbours,
    owner,
    pairing,
    source,
    decay,
    couple,
    faces,
    pick,
    halo,
    source_out,
    decay_out,
    couple_out,
):
    source_out[...] = source[...]
    decay_out[...] = decay[...]
    couple_out[...] = couple[...]
    at = iota((ELEMENTS, WIDTH), 0)

    def chosen(condition):
        return jnp.where(condition, 1.0, 0.0)

    for i in range(2):
        below = jnp.zeros((ELEMENTS, WIDTH), F32)
        for k in range(2):
            below = below + jnp.where(
                (at == owner[1, k]) & (pairing[0, k] == i), 1.0, 0.0
            )
        halo[i] = below
        halo[2 + i] = chosen(at == owner[0, i])
    halo[4] = chosen(at * 0 == pairing[0, 0])
    halo[5] = (at * 0 + mine[0] % RING).astype(F32)
    halo[6] = (at * 0 + mine[0] // RING).astype(F32)

    row = iota((4 * 2 * SLABS, 2 * ROWS), 0)
    col = iota((4 * 2 * SLABS, 2 * ROWS), 1)
    slot = row // (2 * SLABS)
    element = jnp.where(
        slot < 2,
        jnp.where(slot == 0, owner[0, 0], owner[0, 1]),
        jnp.where(slot == 2, owner[1, 0], owner[1, 1]),
    )
    pick[...] = chosen((row % (2 * SLABS)) * ELEMENTS + element == col).astype(BF16)

    e = iota((2 * ELEMENTS, 128), 1) % ELEMENTS
    d = iota((2 * ELEMENTS, 128), 0) % ELEMENTS
    for f in range(FACES):
        to = e
        if f > 0:
            for k in range(ELEMENTS):
                to = jnp.where(e == k, neighbours[f - 1, k], to)
        faces[f] = chosen(to == d).astype(BF16)


def line_kernel(first, *refs):
    if first:
        halo, maps, out, later = refs
        offset_of = lambda j: maps[j, ELEMENTS:]
    else:
        halo, maps, offsets, out, later = refs
        offset_of = lambda j: offsets[j]
    mine = halo[5]
    product = jnp.ones((ELEMENTS, WIDTH), F32)
    offset = jnp.zeros((ELEMENTS, WIDTH), F32)
    for j in reversed(range(RING)):
        if j < RING - 1:
            after = mine == j
            keep = jnp.where(after, offset, keep)
            keep_product = jnp.where(after, product, keep_product)
        else:
            keep, keep_product = offset, product
        offset = offset_of(j) + maps[j, 0:ELEMENTS] * offset
        product = product * maps[j, 0:ELEMENTS]
    if first:
        later[0:ELEMENTS] = keep_product
        later[ELEMENTS:] = keep
        for j in range(LINES):
            out[j, 0:ELEMENTS] = product
            out[j, ELEMENTS:] = offset
    else:
        later[...] = keep
        for j in range(LINES):
            out[j] = offset


def chain_kernel(first, *refs):
    if first:
        field, decay, lines, later = refs[:4]
        refs = refs[4:]
        offset_of = lambda j: lines[j, ELEMENTS:]
        later_offset = later[ELEMENTS:]
    else:
        field, decay, lines, later, line_offsets, later_offsets = refs[:6]
        refs = refs[6:]
        offset_of = lambda j: line_offsets[j]
        later_offset = later_offsets[...]
    pick, halo, couple, chained, spread, up, down = refs

    product = jnp.ones((ELEMENTS, WIDTH), F32)
    offset = jnp.zeros((ELEMENTS, WIDTH), F32)
    for j in reversed(range(LINES)):
        offset = offset_of(j) + lines[j, 0:ELEMENTS] * offset
        product = product * lines[j, 0:ELEMENTS]
    value = offset / (1.0 - product)
    for j in reversed(range(1, LINES)):
        value = jnp.where(halo[6] < j, offset_of(j) + lines[j, 0:ELEMENTS] * value, value)
    value = later_offset + later[0:ELEMENTS] * value
    for t in reversed(range(SLABS)):
        value = field[t] + decay[t] * value
        chained[t] = value
    z = chained[...].reshape(ROWS, WIDTH)
    high = z.astype(BF16)
    low = (z - high.astype(F32)).astype(BF16)
    parts = jnp.concatenate([high, low], axis=0)

    picked = jnp.dot(pick[...], parts, preferred_element_type=F32).astype(BF16)
    products = []
    for k in range(4):
        both = jnp.dot(
            picked[k * 2 * SLABS : (k + 1) * 2 * SLABS],
            couple[k // 2, k % 2],
            preferred_element_type=F32,
        )
        products.append(both[:SLABS] + both[SLABS:])
    up[0] = products[0]
    up[1] = products[1]
    straight = halo[4] > 0.5
    down[0] = jnp.where(straight, products[2], products[3])
    down[1] = jnp.where(straight, products[3], products[2])

    same = jnp.where(iota((128, 128), 0) // 8 == iota((128, 128), 1) // 8, 1.0, 0.0).astype(BF16)
    own = iota((2 * ROWS, DEPTH), 0) % ELEMENTS == iota((2 * ROWS, DEPTH), 1) % ELEMENTS
    n = iota((256, SPAN), 0)
    lane = iota((256, SPAN), 1)
    for b in range(2):
        expand = jnp.where(n == 2 * (lane // ELEMENTS) + b, 1.0, 0.0).astype(BF16)
        wide = jnp.concatenate(
            [
                jnp.dot(parts[:, :256], expand, preferred_element_type=F32),
                jnp.dot(parts[:, 256:], expand[:64, :256], preferred_element_type=F32),
            ],
            axis=1,
        )
        wide = jnp.where(own, wide, 0.0).astype(BF16)
        spread[b * 2 * ROWS : (b + 1) * 2 * ROWS] = jnp.dot(
            same, wide, preferred_element_type=F32
        ).astype(BF16)


def local_kernel(resident, *refs):
    if resident:
        spread, faces, weights, local, low, middle, high = refs
    else:
        spread, faces, stored, local, weights, low, middle, high, sems = refs
        copies = [
            pltpu.make_async_copy(stored.at[f], weights.at[f], sems.at[f]) for f in range(FACES)
        ]
        for copy in copies:
            copy.start()
    half = 2 * ROWS
    for f in range(FACES):
        mask = jnp.concatenate([faces[f]] * (DEPTH // 128), axis=1)
        mask = jnp.concatenate([mask] * (4 * ROWS // 16), axis=0)
        left = spread[...] * mask
        if not resident:
            copies[f].wait()
        parts = (
            (low, left[:half], slice(0, 256)),
            (middle, left, slice(256, 384)),
            (high, left[half:], slice(384, LANES)),
        )
        for sums, rows, lanes in parts:
            part = jnp.dot(rows, weights[f, :, lanes], preferred_element_type=F32)
            if f == 0:
                sums[...] = part
            else:
                sums[...] += part
    even = low[:ROWS] + low[ROWS:]
    even_end = middle[:ROWS] + middle[ROWS:half]
    odd_start = middle[half : half + ROWS] + middle[half + ROWS :]
    odd = high[:ROWS] + high[ROWS:]
    result = jnp.concatenate([even, even_end[:, :64]], axis=1) + jnp.concatenate(
        [odd_start[:, 64:], odd], axis=1
    )
    local[...] = result.reshape(SLABS, ELEMENTS, WIDTH)


def along(x, groups):
    return lax.all_to_all(x, "tm", 0, 0, axis_index_groups=groups, tiled=True)


def operate(first, field, decay, start, known, tables, weights, couple):
    faces, pick, halo = tables
    depth = 2 * ELEMENTS if first else ELEMENTS
    along_z = [[y * RING + z for z in range(RING)] for y in range(LINES)]
    along_y = [[y * RING + z for y in range(LINES)] for z in range(RING)]

    def compose(*refs):
        line_kernel(first, *refs)

    def chain(*refs):
        chain_kernel(first, *refs)

    gathered = along(start, along_z)
    own = (gathered,) if first else (known[0], gathered)
    line, later = pl.pallas_call(
        compose,
        out_shape=(struct(LINES, depth, WIDTH), struct(depth, WIDTH)),
        in_specs=[VMEM] * (1 + len(own)),
        out_specs=(VMEM,) * 2,
        compiler_params=params(SMALL_MIB),
        cost_estimate=pl.CostEstimate(flops=10 * 10**9, bytes_accessed=2 * 10**6, transcendentals=0),
    )(halo, *own)
    lines = along(line, along_y)
    if first:
        known = (gathered, lines, later)
    chained, spread, up, down = pl.pallas_call(
        chain,
        out_shape=(
            struct(SLABS, ELEMENTS, WIDTH),
            jax.ShapeDtypeStruct((4 * ROWS, DEPTH), BF16),
            struct(2, SLABS, WIDTH),
            struct(2, SLABS, WIDTH),
        ),
        in_specs=[VMEM] * (7 if first else 9),
        out_specs=(VMEM,) * 4,
        compiler_params=params(OPERATE_MIB),
        cost_estimate=pl.CostEstimate(flops=10 * 10**9, bytes_accessed=2 * 10**6, transcendentals=0),
    )(field, decay, *known[1:], *(() if first else (lines, later)), pick, halo, couple)
    below = lax.ppermute(up, "space", [(i, (i + 1) % 8) for i in range(8)])
    above = lax.ppermute(down, "space", [((i + 1) % 8, i) for i in range(8)])
    resident = RESIDENT[0 if first else 1]

    def local_part(*refs):
        local_kernel(resident, *refs)

    scratch = [
        pltpu.VMEM((2 * ROWS, 256), F32),
        pltpu.VMEM((4 * ROWS, 128), F32),
        pltpu.VMEM((2 * ROWS, 256), F32),
    ]
    if not resident:
        scratch = [
            pltpu.VMEM((FACES, DEPTH, LANES), BF16),
            *scratch,
            pltpu.SemaphoreType.DMA((FACES,)),
        ]
    local = pl.pallas_call(
        local_part,
        out_shape=struct(SLABS, ELEMENTS, WIDTH),
        in_specs=[VMEM] * 2 + [VMEM if resident else HBM],
        out_specs=VMEM,
        scratch_shapes=scratch,
        compiler_params=params(OPERATE_MIB if resident else WIDE_MIB),
        cost_estimate=pl.CostEstimate(
            flops=2 * FACES * 4 * ROWS * DEPTH * LANES,
            bytes_accessed=2 * FACES * DEPTH * LANES,
            transcendentals=0,
        ),
    )(spread, faces, weights)
    return chained, local, below, above, known


def add_halo(halo, local, below, above, out):
    for t in range(SLABS):
        value = local[t]
        for k in range(2):
            value = value + halo[k] * below[k, t : t + 1]
            value = value + halo[2 + k] * above[k, t : t + 1]
        out[t] = value


def middle_kernel(halo, local, below, above, decay, image, out):
    add_halo(halo, local, below, above, image)
    offset = jnp.zeros((ELEMENTS, WIDTH), F32)
    for t in reversed(range(SLABS)):
        offset = image[t] + decay[t] * offset
    for j in range(RING):
        out[j] = offset


def total_of(x):
    return jnp.sum(jnp.sum(x, axis=0), keepdims=True)


def gram_kernel(halo, local, below, above, source, image0, image1, out):
    add_halo(halo, local, below, above, image1)
    s = source[...]
    largest = [
        jnp.maximum(jnp.max(jnp.max(jnp.abs(image[...]), axis=0), keepdims=True), TINY)
        for image in (image0, image1)
    ]
    one = jnp.ones((1, 1), F32)
    g0 = image0[...] * (1.0 / largest[0])
    g1 = image1[...] * (1.0 / largest[1])
    entries = [
        (total_of(s * s), one, one),
        (total_of(s * g0), largest[0], one),
        (total_of(g0 * g0), largest[0], largest[0]),
        (total_of(s * g1), largest[1], one),
        (total_of(g0 * g1), largest[0], largest[1]),
        (total_of(g1 * g1), largest[1], largest[1]),
    ]
    lane = iota((8, 128), 1)
    row = jnp.ones((8, 128), F32)
    for k, entry in enumerate(entries):
        for i, value in enumerate(entry):
            row = jnp.where(lane == k + 16 * i, value, row)
    for j in range(DEVICES // 8):
        out[j * 8 : (j + 1) * 8] = row


def last_kernel(gram, source, first_chain, second_chain, image0, image1, adjoint, residual):
    every = gram[...]
    scale_a = pltpu.roll(every, 128 - 16, 1)
    scale_b = pltpu.roll(every, 128 - 32, 1)
    top_a = jnp.max(scale_a, axis=0, keepdims=True)
    top_b = jnp.max(scale_b, axis=0, keepdims=True)
    sums = jnp.sum(every * (scale_a / top_a) * (scale_b / top_b), axis=0, keepdims=True)
    lane = iota((1, 128), 1)

    def entry(row, k):
        return jnp.sum(jnp.where(lane == k, row, 0.0), axis=1, keepdims=True)

    ss, s0, g00, s1, g01, g11 = (entry(sums, k) for k in range(6))
    a0 = entry(top_a, 1)
    a1 = entry(top_a, 3)
    square = ss + EPSILON
    norm = jnp.sqrt(square)
    r0 = a0 / norm
    kappa = EPSILON / square - r0 * (s0 / norm)
    rest = r0 * r0 * g00 + 2.0 * kappa * r0 * (s0 / norm) + kappa * kappa * (ss / square)
    h10 = jnp.sqrt(jnp.maximum(rest, 0.0) + EPSILON)
    beta = 1.0 / (norm * h10)
    b0 = r0 / h10
    b1 = (a1 / norm) / h10
    cross = b0 * b1 * g01 + kappa * beta * b1 * s1
    delta = cross + kappa * (b0 * b0 * g00 + kappa * beta * b0 * s0)
    lost = EPSILON / (h10 * h10)
    h00 = 1.0 - kappa
    h11 = (1.0 - lost) + delta
    near = EPSILON * (1.0 - kappa) * beta
    h01 = (b1 * s1 + kappa * b0 * s0 + near) / norm
    c1 = kappa + lost - delta
    mu = (b1 * s1 + beta * EPSILON) / square
    rest = (
        b1 * b1 * g11
        + c1 * c1 * (1.0 - lost)
        + mu * mu * ss
        + 2.0 * c1 * cross
        - 2.0 * mu * b1 * s1
        - 2.0 * c1 * mu * near
    )
    h21 = jnp.sqrt(jnp.maximum(rest, 0.0) + EPSILON)
    radius_one = jnp.sqrt(h00 * h00 + h10 * h10)
    cosine = h00 / radius_one
    sine = h10 / radius_one
    upper = cosine * h01 + sine * h11
    pivot = cosine * h11 - sine * h01
    radius_two = jnp.sqrt(pivot * pivot + h21 * h21)
    y1 = -(norm * sine) * (pivot / radius_two) / radius_two
    y0 = (norm * cosine - upper * y1) / radius_one
    p0 = y0 / norm
    p1 = y1 * beta
    p2 = p1 * kappa
    for t in range(SLABS):
        adjoint[t] = (p0 + p2) * first_chain[t] + p1 * second_chain[t]
        residual[t] = (
            (1.0 - p0 - p2) * source[t] - (p0 + p1 + p2) * image0[t] - p1 * image1[t]
        )


def shards(
    source, decay_rate, blocks, neighbours, interface_jacobian_blocks, face_element_owner, pairing
):
    source = jnp.transpose(source, (0, 2, 1))
    decay = jnp.transpose(decay_rate, (0, 2, 1))
    weights = jnp.transpose(blocks, (1, 0, 2)).reshape(FACES, ELEMENTS, PAIRS, LANES)
    weights = jnp.transpose(weights, (0, 2, 1, 3)).reshape(FACES, DEPTH, LANES)
    couple = interface_jacobian_blocks.reshape(2, 2, WIDTH, WIDTH)
    mine = lax.axis_index("tm").astype(jnp.int32).reshape(1)
    field_shape = struct(SLABS, ELEMENTS, WIDTH)
    maps = pl.pallas_call(
        maps_kernel,
        out_shape=struct(RING, 2 * ELEMENTS, WIDTH),
        in_specs=[HBM] * 2,
        out_specs=VMEM,
        scratch_shapes=[pltpu.VMEM((SLABS, ELEMENTS, WIDTH), F32)] * 2
        + [pltpu.SemaphoreType.DMA((2,))],
        compiler_params=params(WHOLE_MIB),
    )(source, decay)
    *tables, source, decay, couple = pl.pallas_call(
        prepare_kernel,
        out_shape=(
            jax.ShapeDtypeStruct((FACES, 2 * ELEMENTS, 128), BF16),
            jax.ShapeDtypeStruct((4 * 2 * SLABS, 2 * ROWS), BF16),
            struct(7, ELEMENTS, WIDTH),
            field_shape,
            field_shape,
            jax.ShapeDtypeStruct((2, 2, WIDTH, WIDTH), BF16),
        ),
        in_specs=[SMEM] * 4 + [VMEM] * 3,
        out_specs=(VMEM,) * 6,
        compiler_params=params(SMALL_MIB),
    )(mine, neighbours, face_element_owner, pairing, source, decay, couple)
    halo = tables[2]
    chain0, local, below, above, known = operate(
        True, source, decay, maps, None, tables, weights, couple
    )
    image0, offsets = pl.pallas_call(
        middle_kernel,
        out_shape=(field_shape, struct(RING, ELEMENTS, WIDTH)),
        in_specs=[VMEM] * 5,
        out_specs=(VMEM,) * 2,
        compiler_params=params(SMALL_MIB),
    )(halo, local, below, above, decay)
    chain1, local, below, above, known = operate(
        False, image0, decay, offsets, known, tables, weights, couple
    )
    image1, gram = pl.pallas_call(
        gram_kernel,
        out_shape=(field_shape, struct(DEVICES, 128)),
        in_specs=[VMEM] * 6,
        out_specs=(VMEM,) * 2,
        compiler_params=params(SMALL_MIB),
    )(halo, local, below, above, source, image0)
    gram = lax.all_to_all(gram, ("tm", "space"), 0, 0, tiled=True)
    adjoint, residual = pl.pallas_call(
        last_kernel,
        out_shape=(field_shape, field_shape),
        in_specs=[VMEM] * 6,
        out_specs=(VMEM,) * 2,
        compiler_params=params(SMALL_MIB),
    )(gram, source, chain0, chain1, image0, image1)
    return (jnp.transpose(adjoint, (0, 2, 1)), jnp.transpose(residual, (0, 2, 1)))


def solution(mesh):
    in_specs = (
        P("tm", None, "space"),
        P("tm", None, "space"),
        P("space", None, None),
        P(None, "space"),
        P(None, "space", None),
        P(None, "space"),
        P("space", None),
    )
    out_specs = (P("tm", None, "space"), P("tm", None, "space"))
    return jax.shard_map(shards, mesh=mesh, in_specs=in_specs, out_specs=out_specs, check_vma=False)
```

```python
import jax
import jax.numpy as jnp
from jax import lax
from jax.experimental import pallas as pl
from jax.experimental.pallas import tpu as pltpu
from jax.sharding import PartitionSpec as P

EPSILON = 1e-06
F32 = jnp.float32
BF16 = jnp.bfloat16
SLABS = 8
ELEMENTS = 8
WIDTH = 320
FACES = 7
ROWS = SLABS * ELEMENTS
PAIRS = WIDTH // 2
DEPTH = PAIRS * ELEMENTS
LANES = 2 * WIDTH
RING = 8
LINES = 4
DEVICES = 256
TINY = 1e-30
SPAN = 1024
SMALL_MIB = 4
OPERATE_MIB = 8
WIDE_MIB = 46
RESIDENT = (True, True)
WHOLE_MIB = 54

VMEM = pl.BlockSpec(memory_space=pltpu.VMEM)
SMEM = pl.BlockSpec(memory_space=pltpu.SMEM)
HBM = pl.BlockSpec(memory_space=pltpu.HBM)

HINT = pl.CostEstimate(flops=10 * 10**9, bytes_accessed=10**6, transcendentals=0)


def iota(shape, dim):
    return lax.broadcasted_iota(jnp.int32, shape, dim)


def struct(*shape):
    return jax.ShapeDtypeStruct(shape, F32)


def params(mib):
    return pltpu.CompilerParams(vmem_limit_bytes=mib * 1024 * 1024)


def maps_kernel(source_ref, decay_ref, out_ref, source, decay, sems):
    copies = [
        pltpu.make_async_copy(source_ref, source, sems.at[0]),
        pltpu.make_async_copy(decay_ref, decay, sems.at[1]),
    ]
    for copy in copies:
        copy.start()
    for copy in copies:
        copy.wait()
    product = jnp.ones((ELEMENTS, WIDTH), F32)
    offset = jnp.zeros((ELEMENTS, WIDTH), F32)
    for t in reversed(range(SLABS)):
        offset = source[t] + decay[t] * offset
        product = product * decay[t]
    for j in range(RING):
        out_ref[j, 0:ELEMENTS] = product
        out_ref[j, ELEMENTS:] = offset


def prepare_kernel(
    mine,
    neighbours,
    owner,
    pairing,
    source,
    decay,
    couple,
    faces,
    pick,
    halo,
    source_out,
    decay_out,
    couple_out,
):
    source_out[...] = source[...]
    decay_out[...] = decay[...]
    couple_out[...] = couple[...]
    at = iota((ELEMENTS, WIDTH), 0)

    def chosen(condition):
        return jnp.where(condition, 1.0, 0.0)

    for i in range(2):
        below = jnp.zeros((ELEMENTS, WIDTH), F32)
        for k in range(2):
            below = below + jnp.where(
                (at == owner[1, k]) & (pairing[0, k] == i), 1.0, 0.0
            )
        halo[i] = below
        halo[2 + i] = chosen(at == owner[0, i])
    halo[4] = chosen(at * 0 == pairing[0, 0])
    halo[5] = (at * 0 + mine[0] % RING).astype(F32)

    row = iota((4 * 2 * SLABS, 2 * ROWS), 0)
    col = iota((4 * 2 * SLABS, 2 * ROWS), 1)
    slot = row // (2 * SLABS)
    element = jnp.where(
        slot < 2,
        jnp.where(slot == 0, owner[0, 0], owner[0, 1]),
        jnp.where(slot == 2, owner[1, 0], owner[1, 1]),
    )
    pick[...] = chosen((row % (2 * SLABS)) * ELEMENTS + element == col).astype(BF16)

    e = iota((2 * ELEMENTS, 128), 1) % ELEMENTS
    d = iota((2 * ELEMENTS, 128), 0) % ELEMENTS
    for f in range(FACES):
        to = e
        if f > 0:
            for k in range(ELEMENTS):
                to = jnp.where(e == k, neighbours[f - 1, k], to)
        faces[f] = chosen(to == d).astype(BF16)


def line_kernel(first, *refs):
    if first:
        halo, maps, out, later = refs
        offset_of = lambda j: maps[j, ELEMENTS:]
    else:
        halo, maps, offsets, out, later = refs
        offset_of = lambda j: offsets[j]
    mine = halo[5]
    product = jnp.ones((ELEMENTS, WIDTH), F32)
    offset = jnp.zeros((ELEMENTS, WIDTH), F32)
    for j in reversed(range(RING)):
        if j < RING - 1:
            after = mine == j
            keep = jnp.where(after, offset, keep)
            keep_product = jnp.where(after, product, keep_product)
        else:
            keep, keep_product = offset, product
        offset = offset_of(j) + maps[j, 0:ELEMENTS] * offset
        product = product * maps[j, 0:ELEMENTS]
    if first:
        later[0:ELEMENTS] = keep_product
        later[ELEMENTS:] = keep
        out[0:ELEMENTS] = product
        out[ELEMENTS:] = offset
    else:
        later[...] = keep
        out[...] = offset


def chain_kernel(first, *refs):
    field, decay = refs[:2]
    later, *lines = refs[2 : 3 + LINES]
    refs = refs[3 + LINES :]
    if first:
        offsets = [line[ELEMENTS:] for line in lines]
        later_offset = later[ELEMENTS:]
    else:
        later_offset, *offsets = [ref[...] for ref in refs[: 1 + LINES]]
        refs = refs[1 + LINES :]
    pick, halo, couple, chained, spread, up, down = refs

    product = lines[0][0:ELEMENTS]
    offset = offsets[0]
    for j in reversed(range(1, LINES)):
        offset = offsets[j] + lines[j][0:ELEMENTS] * offset
        product = product * lines[j][0:ELEMENTS]
    value = later_offset + later[0:ELEMENTS] * (offset / (1.0 - product))
    for t in reversed(range(SLABS)):
        value = field[t] + decay[t] * value
        chained[t] = value
    z = chained[...].reshape(ROWS, WIDTH)
    high = z.astype(BF16)
    low = (z - high.astype(F32)).astype(BF16)
    parts = jnp.concatenate([high, low], axis=0)

    picked = jnp.dot(pick[...], parts, preferred_element_type=F32).astype(BF16)
    products = []
    for k in range(4):
        both = jnp.dot(
            picked[k * 2 * SLABS : (k + 1) * 2 * SLABS],
            couple[k // 2, k % 2],
            preferred_element_type=F32,
        )
        products.append(both[:SLABS] + both[SLABS:])
    up[0] = products[0]
    up[1] = products[1]
    straight = halo[4] > 0.5
    down[0] = jnp.where(straight, products[2], products[3])
    down[1] = jnp.where(straight, products[3], products[2])

    same = jnp.where(iota((128, 128), 0) // 8 == iota((128, 128), 1) // 8, 1.0, 0.0).astype(BF16)
    own = iota((2 * ROWS, DEPTH), 0) % ELEMENTS == iota((2 * ROWS, DEPTH), 1) % ELEMENTS
    n = iota((256, SPAN), 0)
    lane = iota((256, SPAN), 1)
    for b in range(2):
        expand = jnp.where(n == 2 * (lane // ELEMENTS) + b, 1.0, 0.0).astype(BF16)
        wide = jnp.concatenate(
            [
                jnp.dot(parts[:, :256], expand, preferred_element_type=F32),
                jnp.dot(parts[:, 256:], expand[:64, :256], preferred_element_type=F32),
            ],
            axis=1,
        )
        wide = jnp.where(own, wide, 0.0).astype(BF16)
        spread[b * 2 * ROWS : (b + 1) * 2 * ROWS] = jnp.dot(
            same, wide, preferred_element_type=F32
        ).astype(BF16)


def local_kernel(resident, *refs):
    if resident:
        spread, faces, weights, local, low, middle, high = refs
    else:
        spread, faces, stored, local, weights, low, middle, high, sems = refs
        copies = [
            pltpu.make_async_copy(stored.at[f], weights.at[f], sems.at[f]) for f in range(FACES)
        ]
        for copy in copies:
            copy.start()
    half = 2 * ROWS
    for f in range(FACES):
        mask = jnp.concatenate([faces[f]] * (DEPTH // 128), axis=1)
        mask = jnp.concatenate([mask] * (4 * ROWS // 16), axis=0)
        left = spread[...] * mask
        if not resident:
            copies[f].wait()
        parts = (
            (low, left[:half], slice(0, 256)),
            (middle, left, slice(256, 384)),
            (high, left[half:], slice(384, LANES)),
        )
        for sums, rows, lanes in parts:
            part = jnp.dot(rows, weights[f, :, lanes], preferred_element_type=F32)
            if f == 0:
                sums[...] = part
            else:
                sums[...] += part
    even = low[:ROWS] + low[ROWS:]
    even_end = middle[:ROWS] + middle[ROWS:half]
    odd_start = middle[half : half + ROWS] + middle[half + ROWS :]
    odd = high[:ROWS] + high[ROWS:]
    result = jnp.concatenate([even, even_end[:, :64]], axis=1) + jnp.concatenate(
        [odd_start[:, 64:], odd], axis=1
    )
    local[...] = result.reshape(SLABS, ELEMENTS, WIDTH)


def along(x, groups):
    return lax.all_to_all(x, "tm", 0, 0, axis_index_groups=groups, tiled=True)


def operate(first, field, decay, start, known, tables, weights, couple):
    faces, pick, halo = tables
    depth = 2 * ELEMENTS if first else ELEMENTS
    along_z = [[y * RING + z for z in range(RING)] for y in range(LINES)]

    def compose(*refs):
        line_kernel(first, *refs)

    def chain(*refs):
        chain_kernel(first, *refs)

    gathered = along(start, along_z)
    own = (gathered,) if first else (known[0], gathered)
    line, later = pl.pallas_call(
        compose,
        out_shape=(struct(depth, WIDTH), struct(depth, WIDTH)),
        in_specs=[VMEM] * (1 + len(own)),
        out_specs=(VMEM,) * 2,
        compiler_params=params(SMALL_MIB),
        cost_estimate=HINT,
    )(halo, *own)
    count = RING * LINES
    lines = [line] + [
        lax.ppermute(line, "tm", [((i + k * RING) % count, i) for i in range(count)])
        for k in range(1, LINES)
    ]
    if first:
        known = (gathered, later, *lines)
    chained, spread, up, down = pl.pallas_call(
        chain,
        out_shape=(
            struct(SLABS, ELEMENTS, WIDTH),
            jax.ShapeDtypeStruct((4 * ROWS, DEPTH), BF16),
            struct(2, SLABS, WIDTH),
            struct(2, SLABS, WIDTH),
        ),
        in_specs=[VMEM] * ((1 if first else 2) * (1 + LINES) + 5),
        out_specs=(VMEM,) * 4,
        compiler_params=params(OPERATE_MIB),
        cost_estimate=HINT,
    )(field, decay, *known[1:], *(() if first else (later, *lines)), pick, halo, couple)
    below = lax.ppermute(up, "space", [(i, (i + 1) % 8) for i in range(8)])
    above = lax.ppermute(down, "space", [((i + 1) % 8, i) for i in range(8)])
    resident = RESIDENT[0 if first else 1]

    def local_part(*refs):
        local_kernel(resident, *refs)

    scratch = [
        pltpu.VMEM((2 * ROWS, 256), F32),
        pltpu.VMEM((4 * ROWS, 128), F32),
        pltpu.VMEM((2 * ROWS, 256), F32),
    ]
    if not resident:
        scratch = [
            pltpu.VMEM((FACES, DEPTH, LANES), BF16),
            *scratch,
            pltpu.SemaphoreType.DMA((FACES,)),
        ]
    local = pl.pallas_call(
        local_part,
        out_shape=struct(SLABS, ELEMENTS, WIDTH),
        in_specs=[VMEM] * 2 + [VMEM if resident else HBM],
        out_specs=VMEM,
        scratch_shapes=scratch,
        compiler_params=params(OPERATE_MIB if resident else WIDE_MIB),
        cost_estimate=pl.CostEstimate(
            flops=2 * FACES * 4 * ROWS * DEPTH * LANES,
            bytes_accessed=2 * FACES * DEPTH * LANES,
            transcendentals=0,
        ),
    )(spread, faces, weights)
    return chained, local, below, above, known


def add_halo(halo, local, below, above, out):
    for t in range(SLABS):
        value = local[t]
        for k in range(2):
            value = value + halo[k] * below[k, t : t + 1]
            value = value + halo[2 + k] * above[k, t : t + 1]
        out[t] = value


def middle_kernel(halo, local, below, above, decay, image, out):
    add_halo(halo, local, below, above, image)
    offset = jnp.zeros((ELEMENTS, WIDTH), F32)
    for t in reversed(range(SLABS)):
        offset = image[t] + decay[t] * offset
    for j in range(RING):
        out[j] = offset


def total_of(x):
    return jnp.sum(jnp.sum(x, axis=0), keepdims=True)


def gram_kernel(halo, local, below, above, source, image0, image1, out):
    add_halo(halo, local, below, above, image1)
    s = source[...]
    largest = [
        jnp.maximum(jnp.max(jnp.max(jnp.abs(image[...]), axis=0), keepdims=True), TINY)
        for image in (image0, image1)
    ]
    one = jnp.ones((1, 1), F32)
    g0 = image0[...] * (1.0 / largest[0])
    g1 = image1[...] * (1.0 / largest[1])
    entries = [
        (total_of(s * s), one, one),
        (total_of(s * g0), largest[0], one),
        (total_of(g0 * g0), largest[0], largest[0]),
        (total_of(s * g1), largest[1], one),
        (total_of(g0 * g1), largest[0], largest[1]),
        (total_of(g1 * g1), largest[1], largest[1]),
    ]
    lane = iota((8, 128), 1)
    row = jnp.ones((8, 128), F32)
    for k, entry in enumerate(entries):
        for i, value in enumerate(entry):
            row = jnp.where(lane == k + 16 * i, value, row)
    for j in range(DEVICES // 8):
        out[j * 8 : (j + 1) * 8] = row


def last_kernel(gram, source, first_chain, second_chain, image0, image1, adjoint, residual):
    every = gram[...]
    scale_a = pltpu.roll(every, 128 - 16, 1)
    scale_b = pltpu.roll(every, 128 - 32, 1)
    top_a = jnp.max(scale_a, axis=0, keepdims=True)
    top_b = jnp.max(scale_b, axis=0, keepdims=True)
    sums = jnp.sum(every * (scale_a / top_a) * (scale_b / top_b), axis=0, keepdims=True)
    lane = iota((1, 128), 1)

    def entry(row, k):
        return jnp.sum(jnp.where(lane == k, row, 0.0), axis=1, keepdims=True)

    ss, s0, g00, s1, g01, g11 = (entry(sums, k) for k in range(6))
    a0 = entry(top_a, 1)
    a1 = entry(top_a, 3)
    square = ss + EPSILON
    norm = jnp.sqrt(square)
    r0 = a0 / norm
    kappa = EPSILON / square - r0 * (s0 / norm)
    rest = r0 * r0 * g00 + 2.0 * kappa * r0 * (s0 / norm) + kappa * kappa * (ss / square)
    h10 = jnp.sqrt(jnp.maximum(rest, 0.0) + EPSILON)
    beta = 1.0 / (norm * h10)
    b0 = r0 / h10
    b1 = (a1 / norm) / h10
    cross = b0 * b1 * g01 + kappa * beta * b1 * s1
    delta = cross + kappa * (b0 * b0 * g00 + kappa * beta * b0 * s0)
    lost = EPSILON / (h10 * h10)
    h00 = 1.0 - kappa
    h11 = (1.0 - lost) + delta
    near = EPSILON * (1.0 - kappa) * beta
    h01 = (b1 * s1 + kappa * b0 * s0 + near) / norm
    c1 = kappa + lost - delta
    mu = (b1 * s1 + beta * EPSILON) / square
    rest = (
        b1 * b1 * g11
        + c1 * c1 * (1.0 - lost)
        + mu * mu * ss
        + 2.0 * c1 * cross
        - 2.0 * mu * b1 * s1
        - 2.0 * c1 * mu * near
    )
    h21 = jnp.sqrt(jnp.maximum(rest, 0.0) + EPSILON)
    radius_one = jnp.sqrt(h00 * h00 + h10 * h10)
    cosine = h00 / radius_one
    sine = h10 / radius_one
    upper = cosine * h01 + sine * h11
    pivot = cosine * h11 - sine * h01
    radius_two = jnp.sqrt(pivot * pivot + h21 * h21)
    y1 = -(norm * sine) * (pivot / radius_two) / radius_two
    y0 = (norm * cosine - upper * y1) / radius_one
    p0 = y0 / norm
    p1 = y1 * beta
    p2 = p1 * kappa
    for t in range(SLABS):
        adjoint[t] = (p0 + p2) * first_chain[t] + p1 * second_chain[t]
        residual[t] = (
            (1.0 - p0 - p2) * source[t] - (p0 + p1 + p2) * image0[t] - p1 * image1[t]
        )


def shards(
    source, decay_rate, blocks, neighbours, interface_jacobian_blocks, face_element_owner, pairing
):
    source = jnp.transpose(source, (0, 2, 1))
    decay = jnp.transpose(decay_rate, (0, 2, 1))
    weights = jnp.transpose(blocks, (1, 0, 2)).reshape(FACES, ELEMENTS, PAIRS, LANES)
    weights = jnp.transpose(weights, (0, 2, 1, 3)).reshape(FACES, DEPTH, LANES)
    couple = interface_jacobian_blocks.reshape(2, 2, WIDTH, WIDTH)
    mine = lax.axis_index("tm").astype(jnp.int32).reshape(1)
    field_shape = struct(SLABS, ELEMENTS, WIDTH)
    maps = pl.pallas_call(
        maps_kernel,
        out_shape=struct(RING, 2 * ELEMENTS, WIDTH),
        in_specs=[HBM] * 2,
        out_specs=VMEM,
        scratch_shapes=[pltpu.VMEM((SLABS, ELEMENTS, WIDTH), F32)] * 2
        + [pltpu.SemaphoreType.DMA((2,))],
        compiler_params=params(WHOLE_MIB),
        cost_estimate=HINT,
    )(source, decay)
    *tables, source, decay, couple = pl.pallas_call(
        prepare_kernel,
        out_shape=(
            jax.ShapeDtypeStruct((FACES, 2 * ELEMENTS, 128), BF16),
            jax.ShapeDtypeStruct((4 * 2 * SLABS, 2 * ROWS), BF16),
            struct(6, ELEMENTS, WIDTH),
            field_shape,
            field_shape,
            jax.ShapeDtypeStruct((2, 2, WIDTH, WIDTH), BF16),
        ),
        in_specs=[SMEM] * 4 + [VMEM] * 3,
        out_specs=(VMEM,) * 6,
        compiler_params=params(SMALL_MIB),
    )(mine, neighbours, face_element_owner, pairing, source, decay, couple)
    halo = tables[2]
    chain0, local, below, above, known = operate(
        True, source, decay, maps, None, tables, weights, couple
    )
    image0, offsets = pl.pallas_call(
        middle_kernel,
        out_shape=(field_shape, struct(RING, ELEMENTS, WIDTH)),
        in_specs=[VMEM] * 5,
        out_specs=(VMEM,) * 2,
        compiler_params=params(SMALL_MIB),
    )(halo, local, below, above, decay)
    chain1, local, below, above, known = operate(
        False, image0, decay, offsets, known, tables, weights, couple
    )
    image1, gram = pl.pallas_call(
        gram_kernel,
        out_shape=(field_shape, struct(DEVICES, 128)),
        in_specs=[VMEM] * 6,
        out_specs=(VMEM,) * 2,
        compiler_params=params(SMALL_MIB),
    )(halo, local, below, above, source, image0)
    gram = lax.all_to_all(gram, ("tm", "space"), 0, 0, tiled=True)
    adjoint, residual = pl.pallas_call(
        last_kernel,
        out_shape=(field_shape, field_shape),
        in_specs=[VMEM] * 6,
        out_specs=(VMEM,) * 2,
        compiler_params=params(SMALL_MIB),
    )(gram, source, chain0, chain1, image0, image1)
    return (jnp.transpose(adjoint, (0, 2, 1)), jnp.transpose(residual, (0, 2, 1)))


def solution(mesh):
    in_specs = (
        P("tm", None, "space"),
        P("tm", None, "space"),
        P("space", None, None),
        P(None, "space"),
        P(None, "space", None),
        P(None, "space"),
        P("space", None),
    )
    out_specs = (P("tm", None, "space"), P("tm", None, "space"))
    return jax.shard_map(shards, mesh=mesh, in_specs=in_specs, out_specs=out_specs, check_vma=False)
```

```python
import jax
import jax.numpy as jnp
from jax import lax
from jax.experimental import pallas as pl
from jax.experimental.pallas import tpu as pltpu
from jax.sharding import PartitionSpec as P

EPSILON = 1e-06
F32 = jnp.float32
BF16 = jnp.bfloat16
SLABS = 8
ELEMENTS = 8
WIDTH = 320
FACES = 7
ROWS = SLABS * ELEMENTS
PAIRS = WIDTH // 2
DEPTH = PAIRS * ELEMENTS
LANES = 2 * WIDTH
RING = 8
LINES = 4
DEVICES = 256
TINY = 1e-30
SPAN = 1024
SMALL_MIB = 4
OPERATE_MIB = 8
WHOLE_MIB = 54

VMEM = pl.BlockSpec(memory_space=pltpu.VMEM)
SMEM = pl.BlockSpec(memory_space=pltpu.SMEM)
HBM = pl.BlockSpec(memory_space=pltpu.HBM)

HINT = pl.CostEstimate(flops=10 * 10**9, bytes_accessed=10**6, transcendentals=0)


def iota(shape, dim):
    return lax.broadcasted_iota(jnp.int32, shape, dim)


def struct(*shape):
    return jax.ShapeDtypeStruct(shape, F32)


def params(mib):
    return pltpu.CompilerParams(vmem_limit_bytes=mib * 1024 * 1024)


def maps_kernel(source_ref, decay_ref, out_ref, source, decay, sems):
    copies = [
        pltpu.make_async_copy(source_ref, source, sems.at[0]),
        pltpu.make_async_copy(decay_ref, decay, sems.at[1]),
    ]
    for copy in copies:
        copy.start()
    for copy in copies:
        copy.wait()
    product = jnp.ones((ELEMENTS, WIDTH), F32)
    offset = jnp.zeros((ELEMENTS, WIDTH), F32)
    for t in reversed(range(SLABS)):
        offset = source[t] + decay[t] * offset
        product = product * decay[t]
    for j in range(RING):
        out_ref[j, 0:ELEMENTS] = product
        out_ref[j, ELEMENTS:] = offset


def prepare_kernel(
    mine,
    neighbours,
    owner,
    pairing,
    source,
    decay,
    couple,
    faces,
    pick,
    halo,
    source_out,
    decay_out,
    couple_out,
):
    source_out[...] = source[...]
    decay_out[...] = decay[...]
    couple_out[...] = couple[...]
    at = iota((ELEMENTS, WIDTH), 0)

    def chosen(condition):
        return jnp.where(condition, 1.0, 0.0)

    for i in range(2):
        below = jnp.zeros((ELEMENTS, WIDTH), F32)
        for k in range(2):
            below = below + jnp.where(
                (at == owner[1, k]) & (pairing[0, k] == i), 1.0, 0.0
            )
        halo[i] = below
        halo[2 + i] = chosen(at == owner[0, i])
    halo[4] = chosen(at * 0 == pairing[0, 0])
    halo[5] = (at * 0 + mine[0] % RING).astype(F32)

    row = iota((4 * 2 * SLABS, 2 * ROWS), 0)
    col = iota((4 * 2 * SLABS, 2 * ROWS), 1)
    slot = row // (2 * SLABS)
    element = jnp.where(
        slot < 2,
        jnp.where(slot == 0, owner[0, 0], owner[0, 1]),
        jnp.where(slot == 2, owner[1, 0], owner[1, 1]),
    )
    pick[...] = chosen((row % (2 * SLABS)) * ELEMENTS + element == col).astype(BF16)

    shape = (ROWS, (FACES - 1) * ROWS)
    row, col = iota(shape, 0), iota(shape, 1)
    face, e = col // ROWS, col % ELEMENTS
    to = e
    for f in range(FACES - 1):
        for k in range(ELEMENTS):
            to = jnp.where((face == f) & (e == k), neighbours[f, k], to)
    lands = (col % ROWS) // ELEMENTS * ELEMENTS + to == row
    faces[...] = chosen(lands).astype(BF16)


def line_kernel(first, *refs):
    if first:
        halo, maps, out, later = refs
        offset_of = lambda j: maps[j, ELEMENTS:]
    else:
        halo, maps, offsets, out, later = refs
        offset_of = lambda j: offsets[j]
    mine = halo[5]
    product = jnp.ones((ELEMENTS, WIDTH), F32)
    offset = jnp.zeros((ELEMENTS, WIDTH), F32)
    for j in reversed(range(RING)):
        if j < RING - 1:
            after = mine == j
            keep = jnp.where(after, offset, keep)
            keep_product = jnp.where(after, product, keep_product)
        else:
            keep, keep_product = offset, product
        offset = offset_of(j) + maps[j, 0:ELEMENTS] * offset
        product = product * maps[j, 0:ELEMENTS]
    if first:
        later[0:ELEMENTS] = keep_product
        later[ELEMENTS:] = keep
        out[0:ELEMENTS] = product
        out[ELEMENTS:] = offset
    else:
        later[...] = keep
        out[...] = offset


def chain_kernel(first, *refs):
    field, decay = refs[:2]
    later, *lines = refs[2 : 3 + LINES]
    refs = refs[3 + LINES :]
    if first:
        offsets = [line[ELEMENTS:] for line in lines]
        later_offset = later[ELEMENTS:]
    else:
        later_offset, *offsets = [ref[...] for ref in refs[: 1 + LINES]]
        refs = refs[1 + LINES :]
    pick, halo, couple, chained, spread, up, down = refs

    product = lines[0][0:ELEMENTS]
    offset = offsets[0]
    for j in reversed(range(1, LINES)):
        offset = offsets[j] + lines[j][0:ELEMENTS] * offset
        product = product * lines[j][0:ELEMENTS]
    value = later_offset + later[0:ELEMENTS] * (offset / (1.0 - product))
    for t in reversed(range(SLABS)):
        value = field[t] + decay[t] * value
        chained[t] = value
    z = chained[...].reshape(ROWS, WIDTH)
    high = z.astype(BF16)
    low = (z - high.astype(F32)).astype(BF16)
    parts = jnp.concatenate([high, low], axis=0)

    picked = jnp.dot(pick[...], parts, preferred_element_type=F32).astype(BF16)
    products = []
    for k in range(4):
        both = jnp.dot(
            picked[k * 2 * SLABS : (k + 1) * 2 * SLABS],
            couple[k // 2, k % 2],
            preferred_element_type=F32,
        )
        products.append(both[:SLABS] + both[SLABS:])
    up[0] = products[0]
    up[1] = products[1]
    straight = halo[4] > 0.5
    down[0] = jnp.where(straight, products[2], products[3])
    down[1] = jnp.where(straight, products[3], products[2])

    own = iota((2 * ROWS, DEPTH), 0) % ELEMENTS == iota((2 * ROWS, DEPTH), 1) % ELEMENTS
    n = iota((256, SPAN), 0)
    lane = iota((256, SPAN), 1)
    for b in range(2):
        expand = jnp.where(n == 2 * (lane // ELEMENTS) + b, 1.0, 0.0).astype(BF16)
        wide = jnp.concatenate(
            [
                jnp.dot(parts[:, :256], expand, preferred_element_type=F32),
                jnp.dot(parts[:, 256:], expand[:64, :256], preferred_element_type=F32),
            ],
            axis=1,
        )
        spread[b * 2 * ROWS : (b + 1) * 2 * ROWS] = jnp.where(own, wide, 0.0).astype(BF16)


def local_kernel(spread, faces, weights, local):
    half = 2 * ROWS

    def paired(x):
        return x[:ROWS] + x[ROWS:]

    def products(some):
        both = jnp.dot(
            spread[...],
            jnp.concatenate([weights[f, :, 256:384] for f in some], axis=1),
            preferred_element_type=F32,
        )
        results = []
        for i, f in enumerate(some):
            low = jnp.dot(spread[:half], weights[f, :, :256], preferred_element_type=F32)
            high = jnp.dot(spread[half:], weights[f, :, 384:], preferred_element_type=F32)
            even = paired(both[:half, i * 128 : i * 128 + 64])
            odd = paired(both[half:, i * 128 + 64 : (i + 1) * 128])
            results.append(
                jnp.concatenate([paired(low), even], axis=1)
                + jnp.concatenate([odd, paired(high)], axis=1)
            )
        return results

    result = jnp.zeros((ROWS, WIDTH), F32)
    placed = []
    for some in ((1, 2), (3, 4), (5, 6)):
        placed += products(some)
    placed = jnp.concatenate(placed, axis=0)
    high = placed.astype(BF16)
    low = (placed - high.astype(F32)).astype(BF16)
    for part in (high, low):
        result = result + jnp.dot(faces[...], part, preferred_element_type=F32)
    result = result + products((0,))[0]
    local[...] = result.reshape(SLABS, ELEMENTS, WIDTH)


def along(x, groups):
    return lax.all_to_all(x, "tm", 0, 0, axis_index_groups=groups, tiled=True)


def operate(first, field, decay, start, known, tables, weights, couple):
    faces, pick, halo = tables
    depth = 2 * ELEMENTS if first else ELEMENTS
    along_z = [[y * RING + z for z in range(RING)] for y in range(LINES)]

    def compose(*refs):
        line_kernel(first, *refs)

    def chain(*refs):
        chain_kernel(first, *refs)

    gathered = along(start, along_z)
    own = (gathered,) if first else (known[0], gathered)
    line, later = pl.pallas_call(
        compose,
        out_shape=(struct(depth, WIDTH), struct(depth, WIDTH)),
        in_specs=[VMEM] * (1 + len(own)),
        out_specs=(VMEM,) * 2,
        compiler_params=params(SMALL_MIB),
        cost_estimate=HINT,
    )(halo, *own)
    count = RING * LINES
    lines = [line] + [
        lax.ppermute(line, "tm", [((i + k * RING) % count, i) for i in range(count)])
        for k in range(1, LINES)
    ]
    if first:
        known = (gathered, later, *lines)
    chained, spread, up, down = pl.pallas_call(
        chain,
        out_shape=(
            struct(SLABS, ELEMENTS, WIDTH),
            jax.ShapeDtypeStruct((4 * ROWS, DEPTH), BF16),
            struct(2, SLABS, WIDTH),
            struct(2, SLABS, WIDTH),
        ),
        in_specs=[VMEM] * ((1 if first else 2) * (1 + LINES) + 5),
        out_specs=(VMEM,) * 4,
        compiler_params=params(OPERATE_MIB),
        cost_estimate=HINT,
    )(field, decay, *known[1:], *(() if first else (later, *lines)), pick, halo, couple)
    below = lax.ppermute(up, "space", [(i, (i + 1) % 8) for i in range(8)])
    above = lax.ppermute(down, "space", [((i + 1) % 8, i) for i in range(8)])
    local = pl.pallas_call(
        local_kernel,
        out_shape=struct(SLABS, ELEMENTS, WIDTH),
        in_specs=[VMEM] * 3,
        out_specs=VMEM,
        compiler_params=params(OPERATE_MIB),
        cost_estimate=pl.CostEstimate(
            flops=2 * FACES * 4 * ROWS * DEPTH * LANES,
            bytes_accessed=2 * FACES * DEPTH * LANES,
            transcendentals=0,
        ),
    )(spread, faces, weights)
    return chained, local, below, above, known


def add_halo(halo, local, below, above, out):
    for t in range(SLABS):
        value = local[t]
        for k in range(2):
            value = value + halo[k] * below[k, t : t + 1]
            value = value + halo[2 + k] * above[k, t : t + 1]
        out[t] = value


def middle_kernel(halo, local, below, above, decay, image, out):
    add_halo(halo, local, below, above, image)
    offset = jnp.zeros((ELEMENTS, WIDTH), F32)
    for t in reversed(range(SLABS)):
        offset = image[t] + decay[t] * offset
    for j in range(RING):
        out[j] = offset


def total_of(x):
    return jnp.sum(jnp.sum(x, axis=0), keepdims=True)


def gram_kernel(halo, local, below, above, source, image0, image1, out):
    add_halo(halo, local, below, above, image1)
    s = source[...]
    largest = [
        jnp.maximum(jnp.max(jnp.max(jnp.abs(image[...]), axis=0), keepdims=True), TINY)
        for image in (image0, image1)
    ]
    one = jnp.ones((1, 1), F32)
    g0 = image0[...] * (1.0 / largest[0])
    g1 = image1[...] * (1.0 / largest[1])
    entries = [
        (total_of(s * s), one, one),
        (total_of(s * g0), largest[0], one),
        (total_of(g0 * g0), largest[0], largest[0]),
        (total_of(s * g1), largest[1], one),
        (total_of(g0 * g1), largest[0], largest[1]),
        (total_of(g1 * g1), largest[1], largest[1]),
    ]
    lane = iota((8, 128), 1)
    row = jnp.ones((8, 128), F32)
    for k, entry in enumerate(entries):
        for i, value in enumerate(entry):
            row = jnp.where(lane == k + 16 * i, value, row)
    for j in range(DEVICES // 8):
        out[j * 8 : (j + 1) * 8] = row


def last_kernel(gram, source, first_chain, second_chain, image0, image1, adjoint, residual):
    every = gram[...]
    scale_a = pltpu.roll(every, 128 - 16, 1)
    scale_b = pltpu.roll(every, 128 - 32, 1)
    top_a = jnp.max(scale_a, axis=0, keepdims=True)
    top_b = jnp.max(scale_b, axis=0, keepdims=True)
    sums = jnp.sum(every * (scale_a / top_a) * (scale_b / top_b), axis=0, keepdims=True)
    lane = iota((1, 128), 1)

    def entry(row, k):
        return jnp.sum(jnp.where(lane == k, row, 0.0), axis=1, keepdims=True)

    ss, s0, g00, s1, g01, g11 = (entry(sums, k) for k in range(6))
    a0 = entry(top_a, 1)
    a1 = entry(top_a, 3)
    square = ss + EPSILON
    norm = jnp.sqrt(square)
    r0 = a0 / norm
    kappa = EPSILON / square - r0 * (s0 / norm)
    rest = r0 * r0 * g00 + 2.0 * kappa * r0 * (s0 / norm) + kappa * kappa * (ss / square)
    h10 = jnp.sqrt(jnp.maximum(rest, 0.0) + EPSILON)
    beta = 1.0 / (norm * h10)
    b0 = r0 / h10
    b1 = (a1 / norm) / h10
    cross = b0 * b1 * g01 + kappa * beta * b1 * s1
    delta = cross + kappa * (b0 * b0 * g00 + kappa * beta * b0 * s0)
    lost = EPSILON / (h10 * h10)
    h00 = 1.0 - kappa
    h11 = (1.0 - lost) + delta
    near = EPSILON * (1.0 - kappa) * beta
    h01 = (b1 * s1 + kappa * b0 * s0 + near) / norm
    c1 = kappa + lost - delta
    mu = (b1 * s1 + beta * EPSILON) / square
    rest = (
        b1 * b1 * g11
        + c1 * c1 * (1.0 - lost)
        + mu * mu * ss
        + 2.0 * c1 * cross
        - 2.0 * mu * b1 * s1
        - 2.0 * c1 * mu * near
    )
    h21 = jnp.sqrt(jnp.maximum(rest, 0.0) + EPSILON)
    radius_one = jnp.sqrt(h00 * h00 + h10 * h10)
    cosine = h00 / radius_one
    sine = h10 / radius_one
    upper = cosine * h01 + sine * h11
    pivot = cosine * h11 - sine * h01
    radius_two = jnp.sqrt(pivot * pivot + h21 * h21)
    y1 = -(norm * sine) * (pivot / radius_two) / radius_two
    y0 = (norm * cosine - upper * y1) / radius_one
    p0 = y0 / norm
    p1 = y1 * beta
    p2 = p1 * kappa
    for t in range(SLABS):
        adjoint[t] = (p0 + p2) * first_chain[t] + p1 * second_chain[t]
        residual[t] = (
            (1.0 - p0 - p2) * source[t] - (p0 + p1 + p2) * image0[t] - p1 * image1[t]
        )


def shards(
    source, decay_rate, blocks, neighbours, interface_jacobian_blocks, face_element_owner, pairing
):
    source = jnp.transpose(source, (0, 2, 1))
    decay = jnp.transpose(decay_rate, (0, 2, 1))
    weights = jnp.transpose(blocks, (1, 0, 2)).reshape(FACES, ELEMENTS, PAIRS, LANES)
    weights = jnp.transpose(weights, (0, 2, 1, 3)).reshape(FACES, DEPTH, LANES)
    couple = interface_jacobian_blocks.reshape(2, 2, WIDTH, WIDTH)
    mine = lax.axis_index("tm").astype(jnp.int32).reshape(1)
    field_shape = struct(SLABS, ELEMENTS, WIDTH)
    maps = pl.pallas_call(
        maps_kernel,
        out_shape=struct(RING, 2 * ELEMENTS, WIDTH),
        in_specs=[HBM] * 2,
        out_specs=VMEM,
        scratch_shapes=[pltpu.VMEM((SLABS, ELEMENTS, WIDTH), F32)] * 2
        + [pltpu.SemaphoreType.DMA((2,))],
        compiler_params=params(WHOLE_MIB),
        cost_estimate=HINT,
    )(source, decay)
    *tables, source, decay, couple = pl.pallas_call(
        prepare_kernel,
        out_shape=(
            jax.ShapeDtypeStruct((ROWS, (FACES - 1) * ROWS), BF16),
            jax.ShapeDtypeStruct((4 * 2 * SLABS, 2 * ROWS), BF16),
            struct(6, ELEMENTS, WIDTH),
            field_shape,
            field_shape,
            jax.ShapeDtypeStruct((2, 2, WIDTH, WIDTH), BF16),
        ),
        in_specs=[SMEM] * 4 + [VMEM] * 3,
        out_specs=(VMEM,) * 6,
        compiler_params=params(SMALL_MIB),
    )(mine, neighbours, face_element_owner, pairing, source, decay, couple)
    halo = tables[2]
    chain0, local, below, above, known = operate(
        True, source, decay, maps, None, tables, weights, couple
    )
    image0, offsets = pl.pallas_call(
        middle_kernel,
        out_shape=(field_shape, struct(RING, ELEMENTS, WIDTH)),
        in_specs=[VMEM] * 5,
        out_specs=(VMEM,) * 2,
        compiler_params=params(SMALL_MIB),
    )(halo, local, below, above, decay)
    chain1, local, below, above, known = operate(
        False, image0, decay, offsets, known, tables, weights, couple
    )
    image1, gram = pl.pallas_call(
        gram_kernel,
        out_shape=(field_shape, struct(DEVICES, 128)),
        in_specs=[VMEM] * 6,
        out_specs=(VMEM,) * 2,
        compiler_params=params(SMALL_MIB),
    )(halo, local, below, above, source, image0)
    gram = lax.all_to_all(gram, ("tm", "space"), 0, 0, tiled=True)
    adjoint, residual = pl.pallas_call(
        last_kernel,
        out_shape=(field_shape, field_shape),
        in_specs=[VMEM] * 6,
        out_specs=(VMEM,) * 2,
        compiler_params=params(SMALL_MIB),
    )(gram, source, chain0, chain1, image0, image1)
    return (jnp.transpose(adjoint, (0, 2, 1)), jnp.transpose(residual, (0, 2, 1)))


def solution(mesh):
    in_specs = (
        P("tm", None, "space"),
        P("tm", None, "space"),
        P("space", None, None),
        P(None, "space"),
        P(None, "space", None),
        P(None, "space"),
        P("space", None),
    )
    out_specs = (P("tm", None, "space"), P("tm", None, "space"))
    return jax.shard_map(shards, mesh=mesh, in_specs=in_specs, out_specs=out_specs, check_vma=False)
```

```python
import jax
import jax.numpy as jnp
from jax import lax
from jax.experimental import pallas as pl
from jax.experimental.pallas import tpu as pltpu
from jax.sharding import PartitionSpec as P

EPSILON = 1e-06
F32 = jnp.float32
BF16 = jnp.bfloat16
SLABS = 8
ELEMENTS = 8
WIDTH = 320
FACES = 7
ROWS = SLABS * ELEMENTS
PAIRS = WIDTH // 2
DEPTH = PAIRS * ELEMENTS
LANES = 2 * WIDTH
RING = 8
LINES = 4
DEVICES = 256
TINY = 1e-30
SPAN = 1024
SMALL_MIB = 4
OPERATE_MIB = 8
WHOLE_MIB = 54

VMEM = pl.BlockSpec(memory_space=pltpu.VMEM)
SMEM = pl.BlockSpec(memory_space=pltpu.SMEM)
HBM = pl.BlockSpec(memory_space=pltpu.HBM)

HINT = pl.CostEstimate(flops=10 * 10**9, bytes_accessed=10**6, transcendentals=0)


def iota(shape, dim):
    return lax.broadcasted_iota(jnp.int32, shape, dim)


def struct(*shape):
    return jax.ShapeDtypeStruct(shape, F32)


def params(mib):
    return pltpu.CompilerParams(vmem_limit_bytes=mib * 1024 * 1024)


def maps_kernel(source_ref, decay_ref, out_ref, source, decay, sems):
    copies = [
        pltpu.make_async_copy(source_ref, source, sems.at[0]),
        pltpu.make_async_copy(decay_ref, decay, sems.at[1]),
    ]
    for copy in copies:
        copy.start()
    for copy in copies:
        copy.wait()
    product = jnp.ones((ELEMENTS, WIDTH), F32)
    offset = jnp.zeros((ELEMENTS, WIDTH), F32)
    for t in reversed(range(SLABS)):
        offset = source[t] + decay[t] * offset
        product = product * decay[t]
    for j in range(RING):
        out_ref[j, 0:ELEMENTS] = product
        out_ref[j, ELEMENTS:] = offset


def prepare_kernel(
    mine,
    neighbours,
    owner,
    pairing,
    source,
    decay,
    couple,
    faces,
    pick,
    halo,
    source_out,
    decay_out,
    couple_out,
):
    source_out[...] = source[...]
    decay_out[...] = decay[...]
    at = iota((ELEMENTS, WIDTH), 0)

    def chosen(condition):
        return jnp.where(condition, 1.0, 0.0)

    odd = lax.rem(mine[1], 2)
    for i in range(2):
        below = jnp.zeros((ELEMENTS, WIDTH), F32)
        for k in range(2):
            below = below + jnp.where(
                (at == owner[1, k]) & (pairing[0, k] == i), 1.0, 0.0
            )
        above = chosen(at == owner[0, i])
        halo[i] = jnp.where(at * 0 == odd, above, below)
        halo[2 + i] = jnp.where(at * 0 == odd, below, above)
        couple_out[i] = couple[jnp.bitwise_xor(i, odd)]
    straight = at * 0 == pairing[0, 0]
    halo[4] = chosen(straight | (at * 0 == odd))
    halo[5] = chosen(straight | (at * 0 + 1 == odd))
    halo[6] = (at * 0 + lax.rem(mine[0], RING)).astype(F32)
    halo[7] = (at * 0 + lax.rem(mine[0] // RING, 2)).astype(F32)

    row = iota((4 * 2 * SLABS, 2 * ROWS), 0)
    col = iota((4 * 2 * SLABS, 2 * ROWS), 1)
    slot = row // (2 * SLABS)
    slot = jnp.bitwise_xor(slot, 2 * odd)
    element = jnp.where(
        slot < 2,
        jnp.where(slot == 0, owner[0, 0], owner[0, 1]),
        jnp.where(slot == 2, owner[1, 0], owner[1, 1]),
    )
    pick[...] = chosen((row % (2 * SLABS)) * ELEMENTS + element == col).astype(BF16)

    shape = (ROWS, (FACES - 1) * ROWS)
    row, col = iota(shape, 0), iota(shape, 1)
    face, e = col // ROWS, col % ELEMENTS
    to = e
    for f in range(FACES - 1):
        for k in range(ELEMENTS):
            to = jnp.where((face == f) & (e == k), neighbours[f, k], to)
    lands = (col % ROWS) // ELEMENTS * ELEMENTS + to == row
    faces[...] = chosen(lands).astype(BF16)


def line_kernel(first, *refs):
    if first:
        halo, maps, out, later = refs
        offset_of = lambda j: maps[j, ELEMENTS:]
    else:
        halo, maps, offsets, out, later = refs
        offset_of = lambda j: offsets[j]
    mine = halo[6]
    product = jnp.ones((ELEMENTS, WIDTH), F32)
    offset = jnp.zeros((ELEMENTS, WIDTH), F32)
    for j in reversed(range(RING)):
        if j < RING - 1:
            after = mine == j
            keep = jnp.where(after, offset, keep)
            keep_product = jnp.where(after, product, keep_product)
        else:
            keep, keep_product = offset, product
        offset = offset_of(j) + maps[j, 0:ELEMENTS] * offset
        product = product * maps[j, 0:ELEMENTS]
    if first:
        later[0:ELEMENTS] = keep_product
        later[ELEMENTS:] = keep
        out[0:ELEMENTS] = product
        out[ELEMENTS:] = offset
    else:
        later[...] = keep
        out[...] = offset


def chain_kernel(first, *refs):
    field, decay = refs[:2]
    later, *lines = refs[2 : 3 + LINES]
    refs = refs[3 + LINES :]
    if first:
        offsets = [line[ELEMENTS:] for line in lines]
        later_offset = later[ELEMENTS:]
    else:
        later_offset, *offsets = [ref[...] for ref in refs[: 1 + LINES]]
        refs = refs[1 + LINES :]
    pick, halo, couple, chained, spread, mate, other = refs

    turned = halo[7] > 0.5
    products = [line[0:ELEMENTS] for line in lines]
    for part in (products, offsets):
        part[1], part[3] = (
            jnp.where(turned, part[3], part[1]),
            jnp.where(turned, part[1], part[3]),
        )
    product = products[0]
    offset = offsets[0]
    for j in reversed(range(1, LINES)):
        offset = offsets[j] + products[j] * offset
        product = product * products[j]
    value = later_offset + later[0:ELEMENTS] * (offset / (1.0 - product))
    for t in reversed(range(SLABS)):
        value = field[t] + decay[t] * value
        chained[t] = value
    z = chained[...].reshape(ROWS, WIDTH)
    high = z.astype(BF16)
    low = (z - high.astype(F32)).astype(BF16)
    parts = jnp.concatenate([high, low], axis=0)

    picked = jnp.dot(pick[...], parts, preferred_element_type=F32).astype(BF16)
    products = []
    for k in range(4):
        both = jnp.dot(
            picked[k * 2 * SLABS : (k + 1) * 2 * SLABS],
            couple[k // 2, k % 2],
            preferred_element_type=F32,
        )
        products.append(both[:SLABS] + both[SLABS:])
    for k, out in enumerate((mate, other)):
        straight = halo[4 + k] > 0.5
        out[0] = jnp.where(straight, products[2 * k], products[2 * k + 1])
        out[1] = jnp.where(straight, products[2 * k + 1], products[2 * k])

    own = iota((2 * ROWS, DEPTH), 0) % ELEMENTS == iota((2 * ROWS, DEPTH), 1) % ELEMENTS
    n = iota((256, SPAN), 0)
    lane = iota((256, SPAN), 1)
    for b in range(2):
        expand = jnp.where(n == 2 * (lane // ELEMENTS) + b, 1.0, 0.0).astype(BF16)
        wide = jnp.concatenate(
            [
                jnp.dot(parts[:, :256], expand, preferred_element_type=F32),
                jnp.dot(parts[:, 256:], expand[:64, :256], preferred_element_type=F32),
            ],
            axis=1,
        )
        spread[b * 2 * ROWS : (b + 1) * 2 * ROWS] = jnp.where(own, wide, 0.0).astype(BF16)


def local_kernel(spread, faces, weights, local):
    half = 2 * ROWS

    def paired(x):
        return x[:ROWS] + x[ROWS:]

    def products(some):
        both = jnp.dot(
            spread[...],
            jnp.concatenate([weights[f, :, 256:384] for f in some], axis=1),
            preferred_element_type=F32,
        )
        results = []
        for i, f in enumerate(some):
            low = jnp.dot(spread[:half], weights[f, :, :256], preferred_element_type=F32)
            high = jnp.dot(spread[half:], weights[f, :, 384:], preferred_element_type=F32)
            even = paired(both[:half, i * 128 : i * 128 + 64])
            odd = paired(both[half:, i * 128 + 64 : (i + 1) * 128])
            results.append(
                jnp.concatenate([paired(low), even], axis=1)
                + jnp.concatenate([odd, paired(high)], axis=1)
            )
        return results

    result = jnp.zeros((ROWS, WIDTH), F32)
    placed = []
    for some in ((1, 2), (3, 4), (5, 6)):
        placed += products(some)
    placed = jnp.concatenate(placed, axis=0)
    high = placed.astype(BF16)
    low = (placed - high.astype(F32)).astype(BF16)
    for part in (high, low):
        result = result + jnp.dot(faces[...], part, preferred_element_type=F32)
    result = result + products((0,))[0]
    local[...] = result.reshape(SLABS, ELEMENTS, WIDTH)


def along(x, groups):
    return lax.all_to_all(x, "tm", 0, 0, axis_index_groups=groups, tiled=True)


def operate(first, field, decay, start, known, tables, weights, couple):
    faces, pick, halo = tables
    depth = 2 * ELEMENTS if first else ELEMENTS
    along_z = [[y * RING + z for z in range(RING)] for y in range(LINES)]

    def compose(*refs):
        line_kernel(first, *refs)

    def chain(*refs):
        chain_kernel(first, *refs)

    gathered = along(start, along_z)
    own = (gathered,) if first else (known[0], gathered)
    line, later = pl.pallas_call(
        compose,
        out_shape=(struct(depth, WIDTH), struct(depth, WIDTH)),
        in_specs=[VMEM] * (1 + len(own)),
        out_specs=(VMEM,) * 2,
        compiler_params=params(SMALL_MIB),
        cost_estimate=HINT,
    )(halo, *own)
    count = RING * LINES
    lines = [line] + [
        lax.ppermute(line, "tm", [(i ^ (k * RING), i) for i in range(count)])
        for k in range(1, LINES)
    ]
    if first:
        known = (gathered, later, *lines)
    chained, spread, mate, other = pl.pallas_call(
        chain,
        out_shape=(
            struct(SLABS, ELEMENTS, WIDTH),
            jax.ShapeDtypeStruct((4 * ROWS, DEPTH), BF16),
            struct(2, SLABS, WIDTH),
            struct(2, SLABS, WIDTH),
        ),
        in_specs=[VMEM] * ((1 if first else 2) * (1 + LINES) + 5),
        out_specs=(VMEM,) * 4,
        compiler_params=params(OPERATE_MIB),
        cost_estimate=HINT,
    )(field, decay, *known[1:], *(() if first else (later, *lines)), pick, halo, couple)
    pairs = [(i, i ^ 1) for i in range(8)]
    across = [(i, (i + 1 if i % 2 else i - 1) % 8) for i in range(8)]
    mate = lax.ppermute(mate, "space", pairs)
    other = lax.ppermute(other, "space", across)
    local = pl.pallas_call(
        local_kernel,
        out_shape=struct(SLABS, ELEMENTS, WIDTH),
        in_specs=[VMEM] * 3,
        out_specs=VMEM,
        compiler_params=params(OPERATE_MIB),
        cost_estimate=pl.CostEstimate(
            flops=2 * FACES * 4 * ROWS * DEPTH * LANES,
            bytes_accessed=2 * FACES * DEPTH * LANES,
            transcendentals=0,
        ),
    )(spread, faces, weights)
    return chained, local, mate, other, known


def add_halo(halo, local, mate, other, out):
    for t in range(SLABS):
        value = local[t]
        for k in range(2):
            value = value + halo[k] * mate[k, t : t + 1]
            value = value + halo[2 + k] * other[k, t : t + 1]
        out[t] = value


def middle_kernel(halo, local, mate, other, decay, image, out):
    add_halo(halo, local, mate, other, image)
    offset = jnp.zeros((ELEMENTS, WIDTH), F32)
    for t in reversed(range(SLABS)):
        offset = image[t] + decay[t] * offset
    for j in range(RING):
        out[j] = offset


def total_of(x):
    return jnp.sum(jnp.sum(x, axis=0), keepdims=True)


def gram_kernel(halo, local, mate, other, source, image0, image1, out):
    add_halo(halo, local, mate, other, image1)
    s = source[...]
    largest = [
        jnp.maximum(jnp.max(jnp.max(jnp.abs(image[...]), axis=0), keepdims=True), TINY)
        for image in (image0, image1)
    ]
    one = jnp.ones((1, 1), F32)
    g0 = image0[...] * (1.0 / largest[0])
    g1 = image1[...] * (1.0 / largest[1])
    entries = [
        (total_of(s * s), one, one),
        (total_of(s * g0), largest[0], one),
        (total_of(g0 * g0), largest[0], largest[0]),
        (total_of(s * g1), largest[1], one),
        (total_of(g0 * g1), largest[0], largest[1]),
        (total_of(g1 * g1), largest[1], largest[1]),
    ]
    lane = iota((8, 128), 1)
    row = jnp.ones((8, 128), F32)
    for k, entry in enumerate(entries):
        for i, value in enumerate(entry):
            row = jnp.where(lane == k + 16 * i, value, row)
    for j in range(DEVICES // 8):
        out[j * 8 : (j + 1) * 8] = row


def last_kernel(gram, source, first_chain, second_chain, image0, image1, adjoint, residual):
    every = gram[...]
    scale_a = pltpu.roll(every, 128 - 16, 1)
    scale_b = pltpu.roll(every, 128 - 32, 1)
    top_a = jnp.max(scale_a, axis=0, keepdims=True)
    top_b = jnp.max(scale_b, axis=0, keepdims=True)
    sums = jnp.sum(every * (scale_a / top_a) * (scale_b / top_b), axis=0, keepdims=True)
    lane = iota((1, 128), 1)

    def entry(row, k):
        return jnp.sum(jnp.where(lane == k, row, 0.0), axis=1, keepdims=True)

    ss, s0, g00, s1, g01, g11 = (entry(sums, k) for k in range(6))
    a0 = entry(top_a, 1)
    a1 = entry(top_a, 3)
    square = ss + EPSILON
    norm = jnp.sqrt(square)
    r0 = a0 / norm
    kappa = EPSILON / square - r0 * (s0 / norm)
    rest = r0 * r0 * g00 + 2.0 * kappa * r0 * (s0 / norm) + kappa * kappa * (ss / square)
    h10 = jnp.sqrt(jnp.maximum(rest, 0.0) + EPSILON)
    beta = 1.0 / (norm * h10)
    b0 = r0 / h10
    b1 = (a1 / norm) / h10
    cross = b0 * b1 * g01 + kappa * beta * b1 * s1
    delta = cross + kappa * (b0 * b0 * g00 + kappa * beta * b0 * s0)
    lost = EPSILON / (h10 * h10)
    h00 = 1.0 - kappa
    h11 = (1.0 - lost) + delta
    near = EPSILON * (1.0 - kappa) * beta
    h01 = (b1 * s1 + kappa * b0 * s0 + near) / norm
    c1 = kappa + lost - delta
    mu = (b1 * s1 + beta * EPSILON) / square
    rest = (
        b1 * b1 * g11
        + c1 * c1 * (1.0 - lost)
        + mu * mu * ss
        + 2.0 * c1 * cross
        - 2.0 * mu * b1 * s1
        - 2.0 * c1 * mu * near
    )
    h21 = jnp.sqrt(jnp.maximum(rest, 0.0) + EPSILON)
    radius_one = jnp.sqrt(h00 * h00 + h10 * h10)
    cosine = h00 / radius_one
    sine = h10 / radius_one
    upper = cosine * h01 + sine * h11
    pivot = cosine * h11 - sine * h01
    radius_two = jnp.sqrt(pivot * pivot + h21 * h21)
    y1 = -(norm * sine) * (pivot / radius_two) / radius_two
    y0 = (norm * cosine - upper * y1) / radius_one
    p0 = y0 / norm
    p1 = y1 * beta
    p2 = p1 * kappa
    for t in range(SLABS):
        adjoint[t] = (p0 + p2) * first_chain[t] + p1 * second_chain[t]
        residual[t] = (
            (1.0 - p0 - p2) * source[t] - (p0 + p1 + p2) * image0[t] - p1 * image1[t]
        )


def shards(
    source, decay_rate, blocks, neighbours, interface_jacobian_blocks, face_element_owner, pairing
):
    source = jnp.transpose(source, (0, 2, 1))
    decay = jnp.transpose(decay_rate, (0, 2, 1))
    weights = jnp.transpose(blocks, (1, 0, 2)).reshape(FACES, ELEMENTS, PAIRS, LANES)
    weights = jnp.transpose(weights, (0, 2, 1, 3)).reshape(FACES, DEPTH, LANES)
    couple = interface_jacobian_blocks.reshape(2, 2, WIDTH, WIDTH)
    mine = jnp.stack([lax.axis_index("tm"), lax.axis_index("space")]).astype(jnp.int32)
    field_shape = struct(SLABS, ELEMENTS, WIDTH)
    maps = pl.pallas_call(
        maps_kernel,
        out_shape=struct(RING, 2 * ELEMENTS, WIDTH),
        in_specs=[HBM] * 2,
        out_specs=VMEM,
        scratch_shapes=[pltpu.VMEM((SLABS, ELEMENTS, WIDTH), F32)] * 2
        + [pltpu.SemaphoreType.DMA((2,))],
        compiler_params=params(WHOLE_MIB),
        cost_estimate=HINT,
    )(source, decay)
    *tables, source, decay, couple = pl.pallas_call(
        prepare_kernel,
        out_shape=(
            jax.ShapeDtypeStruct((ROWS, (FACES - 1) * ROWS), BF16),
            jax.ShapeDtypeStruct((4 * 2 * SLABS, 2 * ROWS), BF16),
            struct(8, ELEMENTS, WIDTH),
            field_shape,
            field_shape,
            jax.ShapeDtypeStruct((2, 2, WIDTH, WIDTH), BF16),
        ),
        in_specs=[SMEM] * 4 + [VMEM] * 3,
        out_specs=(VMEM,) * 6,
        compiler_params=params(SMALL_MIB),
    )(mine, neighbours, face_element_owner, pairing, source, decay, couple)
    halo = tables[2]
    chain0, local, mate, other, known = operate(
        True, source, decay, maps, None, tables, weights, couple
    )
    image0, offsets = pl.pallas_call(
        middle_kernel,
        out_shape=(field_shape, struct(RING, ELEMENTS, WIDTH)),
        in_specs=[VMEM] * 5,
        out_specs=(VMEM,) * 2,
        compiler_params=params(SMALL_MIB),
    )(halo, local, mate, other, decay)
    chain1, local, mate, other, known = operate(
        False, image0, decay, offsets, known, tables, weights, couple
    )
    image1, gram = pl.pallas_call(
        gram_kernel,
        out_shape=(field_shape, struct(DEVICES, 128)),
        in_specs=[VMEM] * 6,
        out_specs=(VMEM,) * 2,
        compiler_params=params(SMALL_MIB),
    )(halo, local, mate, other, source, image0)
    gram = lax.all_to_all(gram, ("tm", "space"), 0, 0, tiled=True)
    adjoint, residual = pl.pallas_call(
        last_kernel,
        out_shape=(field_shape, field_shape),
        in_specs=[VMEM] * 6,
        out_specs=(VMEM,) * 2,
        compiler_params=params(SMALL_MIB),
    )(gram, source, chain0, chain1, image0, image1)
    return (jnp.transpose(adjoint, (0, 2, 1)), jnp.transpose(residual, (0, 2, 1)))


def solution(mesh):
    in_specs = (
        P("tm", None, "space"),
        P("tm", None, "space"),
        P("space", None, None),
        P(None, "space"),
        P(None, "space", None),
        P(None, "space"),
        P("space", None),
    )
    out_specs = (P("tm", None, "space"), P("tm", None, "space"))
    return jax.shard_map(shards, mesh=mesh, in_specs=in_specs, out_specs=out_specs, check_vma=False)
```

```python
import jax
import jax.numpy as jnp
from jax import lax
from jax.experimental import pallas as pl
from jax.experimental.pallas import tpu as pltpu
from jax.sharding import PartitionSpec as P

EPSILON = 1e-06
F32 = jnp.float32
BF16 = jnp.bfloat16
SLABS = 8
ELEMENTS = 8
WIDTH = 320
FACES = 7
ROWS = SLABS * ELEMENTS
PAIRS = WIDTH // 2
DEPTH = PAIRS * ELEMENTS
LANES = 2 * WIDTH
RING = 8
LINES = 4
DEVICES = 256
TINY = 1e-30
SPAN = 1024
SMALL_MIB = 4
OPERATE_MIB = 8
WHOLE_MIB = 54

VMEM = pl.BlockSpec(memory_space=pltpu.VMEM)
SMEM = pl.BlockSpec(memory_space=pltpu.SMEM)
HBM = pl.BlockSpec(memory_space=pltpu.HBM)

HINT = pl.CostEstimate(flops=10 * 10**9, bytes_accessed=10**6, transcendentals=0)


def iota(shape, dim):
    return lax.broadcasted_iota(jnp.int32, shape, dim)


def struct(*shape):
    return jax.ShapeDtypeStruct(shape, F32)


def params(mib):
    return pltpu.CompilerParams(vmem_limit_bytes=mib * 1024 * 1024)


def maps_kernel(source_ref, decay_ref, out_ref, source, decay, sems):
    copies = [
        pltpu.make_async_copy(source_ref, source, sems.at[0]),
        pltpu.make_async_copy(decay_ref, decay, sems.at[1]),
    ]
    for copy in copies:
        copy.start()
    for copy in copies:
        copy.wait()
    product = jnp.ones((ELEMENTS, WIDTH), F32)
    offset = jnp.zeros((ELEMENTS, WIDTH), F32)
    for t in reversed(range(SLABS)):
        offset = source[t] + decay[t] * offset
        product = product * decay[t]
    for j in range(RING):
        out_ref[j, 0:ELEMENTS] = product
        out_ref[j, ELEMENTS:] = offset


def prepare_kernel(
    mine,
    neighbours,
    owner,
    pairing,
    source,
    decay,
    couple,
    faces,
    pick,
    halo,
    source_out,
    decay_out,
    couple_out,
):
    source_out[...] = source[...]
    decay_out[...] = decay[...]
    at = iota((ELEMENTS, WIDTH), 0)

    def chosen(condition):
        return jnp.where(condition, 1.0, 0.0)

    odd = lax.rem(mine[1], 2)
    for i in range(2):
        below = jnp.zeros((ELEMENTS, WIDTH), F32)
        for k in range(2):
            below = below + jnp.where(
                (at == owner[1, k]) & (pairing[0, k] == i), 1.0, 0.0
            )
        above = chosen(at == owner[0, i])
        halo[i] = jnp.where(at * 0 == odd, above, below)
        halo[2 + i] = jnp.where(at * 0 == odd, below, above)
        couple_out[i] = couple[jnp.bitwise_xor(i, odd)]
    straight = at * 0 == pairing[0, 0]
    halo[4] = chosen(straight | (at * 0 == odd))
    halo[5] = chosen(straight | (at * 0 + 1 == odd))
    halo[6] = (at * 0 + lax.rem(mine[0], RING)).astype(F32)
    halo[7] = (at * 0 + lax.rem(mine[0] // RING, 2)).astype(F32)

    row = iota((4 * 2 * SLABS, 2 * ROWS), 0)
    col = iota((4 * 2 * SLABS, 2 * ROWS), 1)
    slot = row // (2 * SLABS)
    slot = jnp.bitwise_xor(slot, 2 * odd)
    element = jnp.where(
        slot < 2,
        jnp.where(slot == 0, owner[0, 0], owner[0, 1]),
        jnp.where(slot == 2, owner[1, 0], owner[1, 1]),
    )
    pick[...] = chosen((row % (2 * SLABS)) * ELEMENTS + element == col).astype(BF16)

    shape = (ROWS, (FACES - 1) * ROWS)
    row, col = iota(shape, 0), iota(shape, 1)
    face, e = col // ROWS, col % ELEMENTS
    to = e
    for f in range(FACES - 1):
        for k in range(ELEMENTS):
            to = jnp.where((face == f) & (e == k), neighbours[f, k], to)
    lands = (col % ROWS) // ELEMENTS * ELEMENTS + to == row
    faces[...] = chosen(lands).astype(BF16)


def line_kernel(first, *refs):
    if first:
        halo, maps, out, later = refs
        offset_of = lambda j: maps[j, ELEMENTS:]
    else:
        halo, maps, offsets, out, later = refs
        offset_of = lambda j: offsets[j]
    mine = halo[6]
    product = jnp.ones((ELEMENTS, WIDTH), F32)
    offset = jnp.zeros((ELEMENTS, WIDTH), F32)
    for j in reversed(range(RING)):
        if j < RING - 1:
            after = mine == j
            keep = jnp.where(after, offset, keep)
            keep_product = jnp.where(after, product, keep_product)
        else:
            keep, keep_product = offset, product
        offset = offset_of(j) + maps[j, 0:ELEMENTS] * offset
        product = product * maps[j, 0:ELEMENTS]
    if first:
        later[0:ELEMENTS] = keep_product
        later[ELEMENTS:] = keep
        out[0:ELEMENTS] = product
        out[ELEMENTS:] = offset
    else:
        later[...] = keep
        out[...] = offset


def chain_kernel(first, *refs):
    field, decay = refs[:2]
    later, *lines = refs[2 : 3 + LINES]
    refs = refs[3 + LINES :]
    if first:
        offsets = [line[ELEMENTS:] for line in lines]
        later_offset = later[ELEMENTS:]
    else:
        later_offset, *offsets = [ref[...] for ref in refs[: 1 + LINES]]
        refs = refs[1 + LINES :]
    pick, halo, couple, chained, spread, mate, other = refs

    turned = halo[7] > 0.5
    products = [line[0:ELEMENTS] for line in lines]
    for part in (products, offsets):
        part[1], part[3] = (
            jnp.where(turned, part[3], part[1]),
            jnp.where(turned, part[1], part[3]),
        )
    product = products[0]
    offset = offsets[0]
    for j in reversed(range(1, LINES)):
        offset = offsets[j] + products[j] * offset
        product = product * products[j]
    value = later_offset + later[0:ELEMENTS] * (offset / (1.0 - product))
    for t in reversed(range(SLABS)):
        value = field[t] + decay[t] * value
        chained[t] = value
    z = chained[...].reshape(ROWS, WIDTH)
    high = z.astype(BF16)
    low = (z - high.astype(F32)).astype(BF16)
    parts = jnp.concatenate([high, low], axis=0)

    picked = jnp.dot(pick[...], parts, preferred_element_type=F32).astype(BF16)
    products = []
    for k in range(4):
        both = jnp.dot(
            picked[k * 2 * SLABS : (k + 1) * 2 * SLABS],
            couple[k // 2, k % 2],
            preferred_element_type=F32,
        )
        products.append(both[:SLABS] + both[SLABS:])
    for k, out in enumerate((mate, other)):
        straight = halo[4 + k] > 0.5
        out[0] = jnp.where(straight, products[2 * k], products[2 * k + 1])
        out[1] = jnp.where(straight, products[2 * k + 1], products[2 * k])

    own = iota((2 * ROWS, DEPTH), 0) % ELEMENTS == iota((2 * ROWS, DEPTH), 1) % ELEMENTS
    n = iota((256, SPAN), 0)
    lane = iota((256, SPAN), 1)
    for b in range(2):
        expand = jnp.where(n == 2 * (lane // ELEMENTS) + b, 1.0, 0.0).astype(BF16)
        wide = jnp.concatenate(
            [
                jnp.dot(parts[:, :256], expand, preferred_element_type=F32),
                jnp.dot(parts[:, 256:], expand[:64, :256], preferred_element_type=F32),
            ],
            axis=1,
        )
        spread[b * 2 * ROWS : (b + 1) * 2 * ROWS] = jnp.where(own, wide, 0.0).astype(BF16)


def local_kernel(spread, faces, weights, local):
    half = 2 * ROWS

    def paired(x):
        return x[:ROWS] + x[ROWS:]

    def products(some):
        both = jnp.dot(
            spread[...],
            jnp.concatenate([weights[f, :, 256:384] for f in some], axis=1),
            preferred_element_type=F32,
        )
        results = []
        for i, f in enumerate(some):
            low = jnp.dot(spread[:half], weights[f, :, :256], preferred_element_type=F32)
            high = jnp.dot(spread[half:], weights[f, :, 384:], preferred_element_type=F32)
            even = paired(both[:half, i * 128 : i * 128 + 64])
            odd = paired(both[half:, i * 128 + 64 : (i + 1) * 128])
            results.append(
                jnp.concatenate([paired(low), even], axis=1)
                + jnp.concatenate([odd, paired(high)], axis=1)
            )
        return results

    result = jnp.zeros((ROWS, WIDTH), F32)
    placed = []
    for some in ((1, 2), (3, 4), (5, 6)):
        placed += products(some)
    placed = jnp.concatenate(placed, axis=0)
    high = placed.astype(BF16)
    low = (placed - high.astype(F32)).astype(BF16)
    for part in (high, low):
        result = result + jnp.dot(faces[...], part, preferred_element_type=F32)
    result = result + products((0,))[0]
    local[...] = result.reshape(SLABS, ELEMENTS, WIDTH)


def along(x, groups):
    return lax.all_to_all(x, "tm", 0, 0, axis_index_groups=groups, tiled=True)


def operate(first, field, decay, start, known, tables, weights, couple):
    faces, pick, halo = tables
    depth = 2 * ELEMENTS if first else ELEMENTS
    along_z = [[y * RING + z for z in range(RING)] for y in range(LINES)]

    def compose(*refs):
        line_kernel(first, *refs)

    def chain(*refs):
        chain_kernel(first, *refs)

    gathered = along(start, along_z)
    own = (gathered,) if first else (known[0], gathered)
    line, later = pl.pallas_call(
        compose,
        out_shape=(struct(depth, WIDTH), struct(depth, WIDTH)),
        in_specs=[VMEM] * (1 + len(own)),
        out_specs=(VMEM,) * 2,
        compiler_params=params(SMALL_MIB),
        cost_estimate=HINT,
    )(halo, *own)
    count = RING * LINES
    lines = [line] + [
        lax.ppermute(line, "tm", [(i ^ (k * RING), i) for i in range(count)])
        for k in range(1, LINES)
    ]
    if first:
        known = (gathered, later, *lines)
    chained, spread, mate, other = pl.pallas_call(
        chain,
        out_shape=(
            struct(SLABS, ELEMENTS, WIDTH),
            jax.ShapeDtypeStruct((4 * ROWS, DEPTH), BF16),
            struct(2, SLABS, WIDTH),
            struct(2, SLABS, WIDTH),
        ),
        in_specs=[VMEM] * ((1 if first else 2) * (1 + LINES) + 5),
        out_specs=(VMEM,) * 4,
        compiler_params=params(OPERATE_MIB),
        cost_estimate=HINT,
    )(field, decay, *known[1:], *(() if first else (later, *lines)), pick, halo, couple)
    pairs = [(i, i ^ 1) for i in range(8)]
    across = [(i, (i + 1 if i % 2 else i - 1) % 8) for i in range(8)]
    other = lax.ppermute(other, "space", across)
    mate = lax.ppermute(mate, "space", pairs)
    local = pl.pallas_call(
        local_kernel,
        out_shape=struct(SLABS, ELEMENTS, WIDTH),
        in_specs=[VMEM] * 3,
        out_specs=VMEM,
        compiler_params=params(OPERATE_MIB),
        cost_estimate=pl.CostEstimate(
            flops=2 * FACES * 4 * ROWS * DEPTH * LANES,
            bytes_accessed=2 * FACES * DEPTH * LANES,
            transcendentals=0,
        ),
    )(spread, faces, weights)
    return chained, local, mate, other, known


def add_halo(halo, local, mate, other, out):
    for t in range(SLABS):
        value = local[t]
        for k in range(2):
            value = value + halo[k] * mate[k, t : t + 1]
            value = value + halo[2 + k] * other[k, t : t + 1]
        out[t] = value


def middle_kernel(halo, local, other, mate, decay, image, out):
    add_halo(halo, local, mate, other, image)
    offset = jnp.zeros((ELEMENTS, WIDTH), F32)
    for t in reversed(range(SLABS)):
        offset = image[t] + decay[t] * offset
    for j in range(RING):
        out[j] = offset


def total_of(x):
    return jnp.sum(jnp.sum(x, axis=0), keepdims=True)


def gram_kernel(halo, local, other, mate, source, image0, image1, out):
    add_halo(halo, local, mate, other, image1)
    s = source[...]
    largest = [
        jnp.maximum(jnp.max(jnp.max(jnp.abs(image[...]), axis=0), keepdims=True), TINY)
        for image in (image0, image1)
    ]
    one = jnp.ones((1, 1), F32)
    g0 = image0[...] * (1.0 / largest[0])
    g1 = image1[...] * (1.0 / largest[1])
    entries = [
        (total_of(s * s), one, one),
        (total_of(s * g0), largest[0], one),
        (total_of(g0 * g0), largest[0], largest[0]),
        (total_of(s * g1), largest[1], one),
        (total_of(g0 * g1), largest[0], largest[1]),
        (total_of(g1 * g1), largest[1], largest[1]),
    ]
    lane = iota((8, 128), 1)
    row = jnp.ones((8, 128), F32)
    for k, entry in enumerate(entries):
        for i, value in enumerate(entry):
            row = jnp.where(lane == k + 16 * i, value, row)
    for j in range(DEVICES // 8):
        out[j * 8 : (j + 1) * 8] = row


def last_kernel(gram, source, first_chain, second_chain, image0, image1, adjoint, residual):
    every = gram[...]
    scale_a = pltpu.roll(every, 128 - 16, 1)
    scale_b = pltpu.roll(every, 128 - 32, 1)
    top_a = jnp.max(scale_a, axis=0, keepdims=True)
    top_b = jnp.max(scale_b, axis=0, keepdims=True)
    sums = jnp.sum(every * (scale_a / top_a) * (scale_b / top_b), axis=0, keepdims=True)
    lane = iota((1, 128), 1)

    def entry(row, k):
        return jnp.sum(jnp.where(lane == k, row, 0.0), axis=1, keepdims=True)

    ss, s0, g00, s1, g01, g11 = (entry(sums, k) for k in range(6))
    a0 = entry(top_a, 1)
    a1 = entry(top_a, 3)
    square = ss + EPSILON
    norm = jnp.sqrt(square)
    r0 = a0 / norm
    kappa = EPSILON / square - r0 * (s0 / norm)
    rest = r0 * r0 * g00 + 2.0 * kappa * r0 * (s0 / norm) + kappa * kappa * (ss / square)
    h10 = jnp.sqrt(jnp.maximum(rest, 0.0) + EPSILON)
    beta = 1.0 / (norm * h10)
    b0 = r0 / h10
    b1 = (a1 / norm) / h10
    cross = b0 * b1 * g01 + kappa * beta * b1 * s1
    delta = cross + kappa * (b0 * b0 * g00 + kappa * beta * b0 * s0)
    lost = EPSILON / (h10 * h10)
    h00 = 1.0 - kappa
    h11 = (1.0 - lost) + delta
    near = EPSILON * (1.0 - kappa) * beta
    h01 = (b1 * s1 + kappa * b0 * s0 + near) / norm
    c1 = kappa + lost - delta
    mu = (b1 * s1 + beta * EPSILON) / square
    rest = (
        b1 * b1 * g11
        + c1 * c1 * (1.0 - lost)
        + mu * mu * ss
        + 2.0 * c1 * cross
        - 2.0 * mu * b1 * s1
        - 2.0 * c1 * mu * near
    )
    h21 = jnp.sqrt(jnp.maximum(rest, 0.0) + EPSILON)
    radius_one = jnp.sqrt(h00 * h00 + h10 * h10)
    cosine = h00 / radius_one
    sine = h10 / radius_one
    upper = cosine * h01 + sine * h11
    pivot = cosine * h11 - sine * h01
    radius_two = jnp.sqrt(pivot * pivot + h21 * h21)
    y1 = -(norm * sine) * (pivot / radius_two) / radius_two
    y0 = (norm * cosine - upper * y1) / radius_one
    p0 = y0 / norm
    p1 = y1 * beta
    p2 = p1 * kappa
    for t in range(SLABS):
        adjoint[t] = (p0 + p2) * first_chain[t] + p1 * second_chain[t]
        residual[t] = (
            (1.0 - p0 - p2) * source[t] - (p0 + p1 + p2) * image0[t] - p1 * image1[t]
        )


def shards(
    source, decay_rate, blocks, neighbours, interface_jacobian_blocks, face_element_owner, pairing
):
    source = jnp.transpose(source, (0, 2, 1))
    decay = jnp.transpose(decay_rate, (0, 2, 1))
    weights = jnp.transpose(blocks, (1, 0, 2)).reshape(FACES, ELEMENTS, PAIRS, LANES)
    weights = jnp.transpose(weights, (0, 2, 1, 3)).reshape(FACES, DEPTH, LANES)
    couple = interface_jacobian_blocks.reshape(2, 2, WIDTH, WIDTH)
    mine = jnp.stack([lax.axis_index("tm"), lax.axis_index("space")]).astype(jnp.int32)
    field_shape = struct(SLABS, ELEMENTS, WIDTH)
    maps = pl.pallas_call(
        maps_kernel,
        out_shape=struct(RING, 2 * ELEMENTS, WIDTH),
        in_specs=[HBM] * 2,
        out_specs=VMEM,
        scratch_shapes=[pltpu.VMEM((SLABS, ELEMENTS, WIDTH), F32)] * 2
        + [pltpu.SemaphoreType.DMA((2,))],
        compiler_params=params(WHOLE_MIB),
        cost_estimate=HINT,
    )(source, decay)
    *tables, source, decay, couple = pl.pallas_call(
        prepare_kernel,
        out_shape=(
            jax.ShapeDtypeStruct((ROWS, (FACES - 1) * ROWS), BF16),
            jax.ShapeDtypeStruct((4 * 2 * SLABS, 2 * ROWS), BF16),
            struct(8, ELEMENTS, WIDTH),
            field_shape,
            field_shape,
            jax.ShapeDtypeStruct((2, 2, WIDTH, WIDTH), BF16),
        ),
        in_specs=[SMEM] * 4 + [VMEM] * 3,
        out_specs=(VMEM,) * 6,
        compiler_params=params(SMALL_MIB),
    )(mine, neighbours, face_element_owner, pairing, source, decay, couple)
    halo = tables[2]
    chain0, local, mate, other, known = operate(
        True, source, decay, maps, None, tables, weights, couple
    )
    image0, offsets = pl.pallas_call(
        middle_kernel,
        out_shape=(field_shape, struct(RING, ELEMENTS, WIDTH)),
        in_specs=[VMEM] * 5,
        out_specs=(VMEM,) * 2,
        compiler_params=params(SMALL_MIB),
    )(halo, local, other, mate, decay)
    chain1, local, mate, other, known = operate(
        False, image0, decay, offsets, known, tables, weights, couple
    )
    image1, gram = pl.pallas_call(
        gram_kernel,
        out_shape=(field_shape, struct(DEVICES, 128)),
        in_specs=[VMEM] * 6,
        out_specs=(VMEM,) * 2,
        compiler_params=params(SMALL_MIB),
    )(halo, local, other, mate, source, image0)
    gram = lax.all_to_all(gram, ("tm", "space"), 0, 0, tiled=True)
    adjoint, residual = pl.pallas_call(
        last_kernel,
        out_shape=(field_shape, field_shape),
        in_specs=[VMEM] * 6,
        out_specs=(VMEM,) * 2,
        compiler_params=params(SMALL_MIB),
    )(gram, source, chain0, chain1, image0, image1)
    return (jnp.transpose(adjoint, (0, 2, 1)), jnp.transpose(residual, (0, 2, 1)))


def solution(mesh):
    in_specs = (
        P("tm", None, "space"),
        P("tm", None, "space"),
        P("space", None, None),
        P(None, "space"),
        P(None, "space", None),
        P(None, "space"),
        P("space", None),
    )
    out_specs = (P("tm", None, "space"), P("tm", None, "space"))
    return jax.shard_map(shards, mesh=mesh, in_specs=in_specs, out_specs=out_specs, check_vma=False)
```

```python
import jax
import jax.numpy as jnp
from jax import lax
from jax.experimental import pallas as pl
from jax.experimental.pallas import tpu as pltpu
from jax.sharding import PartitionSpec as P

EPSILON = 1e-06
F32 = jnp.float32
BF16 = jnp.bfloat16
SLABS = 8
ELEMENTS = 8
WIDTH = 320
FACES = 7
ROWS = SLABS * ELEMENTS
PAIRS = WIDTH // 2
DEPTH = PAIRS * ELEMENTS
LANES = 2 * WIDTH
RING = 8
LINES = 4
DEVICES = 256
TINY = 1e-30
SPAN = 1024
SMALL_MIB = 4
OPERATE_MIB = 8
WHOLE_MIB = 54

VMEM = pl.BlockSpec(memory_space=pltpu.VMEM)
SMEM = pl.BlockSpec(memory_space=pltpu.SMEM)
HBM = pl.BlockSpec(memory_space=pltpu.HBM)

HINT = pl.CostEstimate(flops=10 * 10**9, bytes_accessed=10**6, transcendentals=0)


def iota(shape, dim):
    return lax.broadcasted_iota(jnp.int32, shape, dim)


def struct(*shape):
    return jax.ShapeDtypeStruct(shape, F32)


def params(mib):
    return pltpu.CompilerParams(vmem_limit_bytes=mib * 1024 * 1024)


def maps_kernel(source_ref, decay_ref, out_ref, source, decay, sems):
    copies = [
        pltpu.make_async_copy(source_ref, source, sems.at[0]),
        pltpu.make_async_copy(decay_ref, decay, sems.at[1]),
    ]
    for copy in copies:
        copy.start()
    for copy in copies:
        copy.wait()
    product = jnp.ones((ELEMENTS, WIDTH), F32)
    offset = jnp.zeros((ELEMENTS, WIDTH), F32)
    for t in reversed(range(SLABS)):
        offset = source[t] + decay[t] * offset
        product = product * decay[t]
    for j in range(RING):
        out_ref[j, 0:ELEMENTS] = product
        out_ref[j, ELEMENTS:] = offset


def prepare_kernel(
    mine,
    neighbours,
    owner,
    pairing,
    source,
    decay,
    couple,
    faces,
    pick,
    halo,
    source_out,
    decay_out,
    couple_out,
):
    source_out[...] = source[...]
    decay_out[...] = decay[...]
    at = iota((ELEMENTS, WIDTH), 0)

    def chosen(condition):
        return jnp.where(condition, 1.0, 0.0)

    odd = lax.rem(mine[1], 2)
    for i in range(2):
        below = jnp.zeros((ELEMENTS, WIDTH), F32)
        for k in range(2):
            below = below + jnp.where(
                (at == owner[1, k]) & (pairing[0, k] == i), 1.0, 0.0
            )
        above = chosen(at == owner[0, i])
        halo[i] = jnp.where(at * 0 == odd, above, below)
        halo[2 + i] = jnp.where(at * 0 == odd, below, above)
        couple_out[i] = couple[jnp.bitwise_xor(i, odd)]
    straight = at * 0 == pairing[0, 0]
    halo[4] = chosen(straight | (at * 0 == odd))
    halo[5] = chosen(straight | (at * 0 + 1 == odd))
    halo[6] = (at * 0 + lax.rem(mine[0], RING)).astype(F32)
    halo[7] = (at * 0 + lax.rem(mine[0] // RING, 2)).astype(F32)

    row = iota((4 * 2 * SLABS, 2 * ROWS), 0)
    col = iota((4 * 2 * SLABS, 2 * ROWS), 1)
    slot = row // (2 * SLABS)
    slot = jnp.bitwise_xor(slot, 2 * odd)
    element = jnp.where(
        slot < 2,
        jnp.where(slot == 0, owner[0, 0], owner[0, 1]),
        jnp.where(slot == 2, owner[1, 0], owner[1, 1]),
    )
    pick[...] = chosen((row % (2 * SLABS)) * ELEMENTS + element == col).astype(BF16)

    shape = (ROWS, (FACES - 1) * ROWS)
    row, col = iota(shape, 0), iota(shape, 1)
    face, e = col // ROWS, col % ELEMENTS
    to = e
    for f in range(FACES - 1):
        for k in range(ELEMENTS):
            to = jnp.where((face == f) & (e == k), neighbours[f, k], to)
    lands = (col % ROWS) // ELEMENTS * ELEMENTS + to == row
    faces[...] = chosen(lands).astype(BF16)


def line_kernel(first, *refs):
    if first:
        halo, maps, out, later = refs
        offset_of = lambda j: maps[j, ELEMENTS:]
    else:
        halo, maps, offsets, out, later = refs
        offset_of = lambda j: offsets[j]
    mine = halo[6]
    product = jnp.ones((ELEMENTS, WIDTH), F32)
    offset = jnp.zeros((ELEMENTS, WIDTH), F32)
    for j in reversed(range(RING)):
        if j < RING - 1:
            after = mine == j
            keep = jnp.where(after, offset, keep)
            keep_product = jnp.where(after, product, keep_product)
        else:
            keep, keep_product = offset, product
        offset = offset_of(j) + maps[j, 0:ELEMENTS] * offset
        product = product * maps[j, 0:ELEMENTS]
    if first:
        later[0:ELEMENTS] = keep_product
        later[ELEMENTS:] = keep
        out[0:ELEMENTS] = product
        out[ELEMENTS:] = offset
    else:
        later[...] = keep
        out[...] = offset


def chain_kernel(first, *refs):
    field, decay = refs[:2]
    later, *lines = refs[2 : 3 + LINES]
    refs = refs[3 + LINES :]
    if first:
        offsets = [line[ELEMENTS:] for line in lines]
        later_offset = later[ELEMENTS:]
    else:
        later_offset, *offsets = [ref[...] for ref in refs[: 1 + LINES]]
        refs = refs[1 + LINES :]
    pick, halo, couple, chained, spread, mate, other = refs

    turned = halo[7] > 0.5
    products = [line[0:ELEMENTS] for line in lines]
    for part in (products, offsets):
        part[1], part[3] = (
            jnp.where(turned, part[3], part[1]),
            jnp.where(turned, part[1], part[3]),
        )
    product = products[0]
    offset = offsets[0]
    for j in reversed(range(1, LINES)):
        offset = offsets[j] + products[j] * offset
        product = product * products[j]
    value = later_offset + later[0:ELEMENTS] * (offset / (1.0 - product))
    for t in reversed(range(SLABS)):
        value = field[t] + decay[t] * value
        chained[t] = value
    z = chained[...].reshape(ROWS, WIDTH)
    high = z.astype(BF16)
    low = (z - high.astype(F32)).astype(BF16)
    parts = jnp.concatenate([high, low], axis=0)

    picked = jnp.dot(pick[...], parts, preferred_element_type=F32).astype(BF16)
    products = []
    for k in range(4):
        both = jnp.dot(
            picked[k * 2 * SLABS : (k + 1) * 2 * SLABS],
            couple[k // 2, k % 2],
            preferred_element_type=F32,
        )
        products.append(both[:SLABS] + both[SLABS:])
    for k, out in enumerate((mate, other)):
        straight = halo[4 + k] > 0.5
        out[0] = jnp.where(straight, products[2 * k], products[2 * k + 1])
        out[1] = jnp.where(straight, products[2 * k + 1], products[2 * k])

    own = iota((2 * ROWS, DEPTH), 0) % ELEMENTS == iota((2 * ROWS, DEPTH), 1) % ELEMENTS
    n = iota((256, SPAN), 0)
    lane = iota((256, SPAN), 1)
    for b in range(2):
        expand = jnp.where(n == 2 * (lane // ELEMENTS) + b, 1.0, 0.0).astype(BF16)
        wide = jnp.concatenate(
            [
                jnp.dot(parts[:, :256], expand, preferred_element_type=F32),
                jnp.dot(parts[:, 256:], expand[:64, :256], preferred_element_type=F32),
            ],
            axis=1,
        )
        spread[b * 2 * ROWS : (b + 1) * 2 * ROWS] = jnp.where(own, wide, 0.0).astype(BF16)


def local_kernel(spread, faces, weights, local):
    half = 2 * ROWS

    def paired(x):
        return x[:ROWS] + x[ROWS:]

    def products(some):
        both = jnp.dot(
            spread[...],
            jnp.concatenate([weights[f, :, 256:384] for f in some], axis=1),
            preferred_element_type=F32,
        )
        results = []
        for i, f in enumerate(some):
            low = jnp.dot(spread[:half], weights[f, :, :256], preferred_element_type=F32)
            high = jnp.dot(spread[half:], weights[f, :, 384:], preferred_element_type=F32)
            even = paired(both[:half, i * 128 : i * 128 + 64])
            odd = paired(both[half:, i * 128 + 64 : (i + 1) * 128])
            results.append(
                jnp.concatenate([paired(low), even], axis=1)
                + jnp.concatenate([odd, paired(high)], axis=1)
            )
        return results

    placed = []
    for some in ((1, 2), (3, 4), (5, 6)):
        placed += products(some)
    result = products((0,))[0]
    placed = jnp.concatenate(placed, axis=0)
    high = placed.astype(BF16)
    low = (placed - high.astype(F32)).astype(BF16)
    for part in (high, low):
        result = result + jnp.dot(faces[...], part, preferred_element_type=F32)
    local[...] = result.reshape(SLABS, ELEMENTS, WIDTH)


def along(x, groups):
    return lax.all_to_all(x, "tm", 0, 0, axis_index_groups=groups, tiled=True)


def operate(first, field, decay, start, known, tables, weights, couple):
    faces, pick, halo = tables
    depth = 2 * ELEMENTS if first else ELEMENTS
    along_z = [[y * RING + z for z in range(RING)] for y in range(LINES)]

    def compose(*refs):
        line_kernel(first, *refs)

    def chain(*refs):
        chain_kernel(first, *refs)

    gathered = along(start, along_z)
    own = (gathered,) if first else (known[0], gathered)
    line, later = pl.pallas_call(
        compose,
        out_shape=(struct(depth, WIDTH), struct(depth, WIDTH)),
        in_specs=[VMEM] * (1 + len(own)),
        out_specs=(VMEM,) * 2,
        compiler_params=params(SMALL_MIB),
        cost_estimate=HINT,
    )(halo, *own)
    count = RING * LINES
    lines = [line] + [
        lax.ppermute(line, "tm", [(i ^ (k * RING), i) for i in range(count)])
        for k in range(1, LINES)
    ]
    if first:
        known = (gathered, later, *lines)
    chained, spread, mate, other = pl.pallas_call(
        chain,
        out_shape=(
            struct(SLABS, ELEMENTS, WIDTH),
            jax.ShapeDtypeStruct((4 * ROWS, DEPTH), BF16),
            struct(2, SLABS, WIDTH),
            struct(2, SLABS, WIDTH),
        ),
        in_specs=[VMEM] * ((1 if first else 2) * (1 + LINES) + 5),
        out_specs=(VMEM,) * 4,
        compiler_params=params(OPERATE_MIB),
        cost_estimate=HINT,
    )(field, decay, *known[1:], *(() if first else (later, *lines)), pick, halo, couple)
    pairs = [(i, i ^ 1) for i in range(8)]
    across = [(i, (i + 1 if i % 2 else i - 1) % 8) for i in range(8)]
    other = lax.ppermute(other, "space", across)
    mate = lax.ppermute(mate, "space", pairs)
    local = pl.pallas_call(
        local_kernel,
        out_shape=struct(SLABS, ELEMENTS, WIDTH),
        in_specs=[VMEM] * 3,
        out_specs=VMEM,
        compiler_params=params(OPERATE_MIB),
        cost_estimate=pl.CostEstimate(
            flops=2 * FACES * 4 * ROWS * DEPTH * LANES,
            bytes_accessed=2 * FACES * DEPTH * LANES,
            transcendentals=0,
        ),
    )(spread, faces, weights)
    return chained, local, mate, other, known


def add_halo(halo, local, mate, other, out):
    for t in range(SLABS):
        value = local[t]
        for k in range(2):
            value = value + halo[k] * mate[k, t : t + 1]
            value = value + halo[2 + k] * other[k, t : t + 1]
        out[t] = value


def middle_kernel(halo, local, other, mate, decay, image, out):
    add_halo(halo, local, mate, other, image)
    offset = jnp.zeros((ELEMENTS, WIDTH), F32)
    for t in reversed(range(SLABS)):
        offset = image[t] + decay[t] * offset
    for j in range(RING):
        out[j] = offset


def total_of(x):
    return jnp.sum(jnp.sum(x, axis=0), keepdims=True)


def gram_kernel(halo, local, other, mate, source, image0, image1, out):
    add_halo(halo, local, mate, other, image1)
    s = source[...]
    largest = [
        jnp.maximum(jnp.max(jnp.max(jnp.abs(image[...]), axis=0), keepdims=True), TINY)
        for image in (image0, image1)
    ]
    one = jnp.ones((1, 1), F32)
    g0 = image0[...] * (1.0 / largest[0])
    g1 = image1[...] * (1.0 / largest[1])
    entries = [
        (total_of(s * s), one, one),
        (total_of(s * g0), largest[0], one),
        (total_of(g0 * g0), largest[0], largest[0]),
        (total_of(s * g1), largest[1], one),
        (total_of(g0 * g1), largest[0], largest[1]),
        (total_of(g1 * g1), largest[1], largest[1]),
    ]
    lane = iota((8, 128), 1)
    row = jnp.ones((8, 128), F32)
    for k, entry in enumerate(entries):
        for i, value in enumerate(entry):
            row = jnp.where(lane == k + 16 * i, value, row)
    for j in range(DEVICES // 8):
        out[j * 8 : (j + 1) * 8] = row


def last_kernel(gram, source, first_chain, second_chain, image0, image1, adjoint, residual):
    every = gram[...]
    scale_a = pltpu.roll(every, 128 - 16, 1)
    scale_b = pltpu.roll(every, 128 - 32, 1)
    top_a = jnp.max(scale_a, axis=0, keepdims=True)
    top_b = jnp.max(scale_b, axis=0, keepdims=True)
    sums = jnp.sum(every * (scale_a / top_a) * (scale_b / top_b), axis=0, keepdims=True)
    lane = iota((1, 128), 1)

    def entry(row, k):
        return jnp.sum(jnp.where(lane == k, row, 0.0), axis=1, keepdims=True)

    ss, s0, g00, s1, g01, g11 = (entry(sums, k) for k in range(6))
    a0 = entry(top_a, 1)
    a1 = entry(top_a, 3)
    square = ss + EPSILON
    norm = jnp.sqrt(square)
    r0 = a0 / norm
    kappa = EPSILON / square - r0 * (s0 / norm)
    rest = r0 * r0 * g00 + 2.0 * kappa * r0 * (s0 / norm) + kappa * kappa * (ss / square)
    h10 = jnp.sqrt(jnp.maximum(rest, 0.0) + EPSILON)
    beta = 1.0 / (norm * h10)
    b0 = r0 / h10
    b1 = (a1 / norm) / h10
    cross = b0 * b1 * g01 + kappa * beta * b1 * s1
    delta = cross + kappa * (b0 * b0 * g00 + kappa * beta * b0 * s0)
    lost = EPSILON / (h10 * h10)
    h00 = 1.0 - kappa
    h11 = (1.0 - lost) + delta
    near = EPSILON * (1.0 - kappa) * beta
    h01 = (b1 * s1 + kappa * b0 * s0 + near) / norm
    c1 = kappa + lost - delta
    mu = (b1 * s1 + beta * EPSILON) / square
    rest = (
        b1 * b1 * g11
        + c1 * c1 * (1.0 - lost)
        + mu * mu * ss
        + 2.0 * c1 * cross
        - 2.0 * mu * b1 * s1
        - 2.0 * c1 * mu * near
    )
    h21 = jnp.sqrt(jnp.maximum(rest, 0.0) + EPSILON)
    radius_one = jnp.sqrt(h00 * h00 + h10 * h10)
    cosine = h00 / radius_one
    sine = h10 / radius_one
    upper = cosine * h01 + sine * h11
    pivot = cosine * h11 - sine * h01
    radius_two = jnp.sqrt(pivot * pivot + h21 * h21)
    y1 = -(norm * sine) * (pivot / radius_two) / radius_two
    y0 = (norm * cosine - upper * y1) / radius_one
    p0 = y0 / norm
    p1 = y1 * beta
    p2 = p1 * kappa
    for t in range(SLABS):
        adjoint[t] = (p0 + p2) * first_chain[t] + p1 * second_chain[t]
        residual[t] = (
            (1.0 - p0 - p2) * source[t] - (p0 + p1 + p2) * image0[t] - p1 * image1[t]
        )


def shards(
    source, decay_rate, blocks, neighbours, interface_jacobian_blocks, face_element_owner, pairing
):
    source = jnp.transpose(source, (0, 2, 1))
    decay = jnp.transpose(decay_rate, (0, 2, 1))
    weights = jnp.transpose(blocks, (1, 0, 2)).reshape(FACES, ELEMENTS, PAIRS, LANES)
    weights = jnp.transpose(weights, (0, 2, 1, 3)).reshape(FACES, DEPTH, LANES)
    couple = interface_jacobian_blocks.reshape(2, 2, WIDTH, WIDTH)
    mine = jnp.stack([lax.axis_index("tm"), lax.axis_index("space")]).astype(jnp.int32)
    field_shape = struct(SLABS, ELEMENTS, WIDTH)
    maps = pl.pallas_call(
        maps_kernel,
        out_shape=struct(RING, 2 * ELEMENTS, WIDTH),
        in_specs=[HBM] * 2,
        out_specs=VMEM,
        scratch_shapes=[pltpu.VMEM((SLABS, ELEMENTS, WIDTH), F32)] * 2
        + [pltpu.SemaphoreType.DMA((2,))],
        compiler_params=params(WHOLE_MIB),
        cost_estimate=HINT,
    )(source, decay)
    *tables, source, decay, couple = pl.pallas_call(
        prepare_kernel,
        out_shape=(
            jax.ShapeDtypeStruct((ROWS, (FACES - 1) * ROWS), BF16),
            jax.ShapeDtypeStruct((4 * 2 * SLABS, 2 * ROWS), BF16),
            struct(8, ELEMENTS, WIDTH),
            field_shape,
            field_shape,
            jax.ShapeDtypeStruct((2, 2, WIDTH, WIDTH), BF16),
        ),
        in_specs=[SMEM] * 4 + [VMEM] * 3,
        out_specs=(VMEM,) * 6,
        compiler_params=params(SMALL_MIB),
    )(mine, neighbours, face_element_owner, pairing, source, decay, couple)
    halo = tables[2]
    chain0, local, mate, other, known = operate(
        True, source, decay, maps, None, tables, weights, couple
    )
    image0, offsets = pl.pallas_call(
        middle_kernel,
        out_shape=(field_shape, struct(RING, ELEMENTS, WIDTH)),
        in_specs=[VMEM] * 5,
        out_specs=(VMEM,) * 2,
        compiler_params=params(SMALL_MIB),
    )(halo, local, other, mate, decay)
    chain1, local, mate, other, known = operate(
        False, image0, decay, offsets, known, tables, weights, couple
    )
    image1, gram = pl.pallas_call(
        gram_kernel,
        out_shape=(field_shape, struct(DEVICES, 128)),
        in_specs=[VMEM] * 6,
        out_specs=(VMEM,) * 2,
        compiler_params=params(SMALL_MIB),
    )(halo, local, other, mate, source, image0)
    gram = lax.all_to_all(gram, ("tm", "space"), 0, 0, tiled=True)
    adjoint, residual = pl.pallas_call(
        last_kernel,
        out_shape=(field_shape, field_shape),
        in_specs=[VMEM] * 6,
        out_specs=(VMEM,) * 2,
        compiler_params=params(SMALL_MIB),
    )(gram, source, chain0, chain1, image0, image1)
    return (jnp.transpose(adjoint, (0, 2, 1)), jnp.transpose(residual, (0, 2, 1)))


def solution(mesh):
    in_specs = (
        P("tm", None, "space"),
        P("tm", None, "space"),
        P("space", None, None),
        P(None, "space"),
        P(None, "space", None),
        P(None, "space"),
        P("space", None),
    )
    out_specs = (P("tm", None, "space"), P("tm", None, "space"))
    return jax.shard_map(shards, mesh=mesh, in_specs=in_specs, out_specs=out_specs, check_vma=False)
```
